32 devices in a mesh: section: 2 (over core), tp: 16 (over z, y, x).
Axes of the slice: x: 2, y: 2, z: 4, core: 2. Of those that a mesh axis runs over, the one named last changes fastest.
Arguments:
- text_states: bfloat16 [128, 8192], P(None, 'tp'), may hold values from -7 to 7
- vision_states: bfloat16 [256, 1280], P('section'), may hold values from -6 to 6
- visible_tiles: int32 [128], replicated, may hold values from 0 to 4
- vision_norm_gain: float32 [1280], replicated, may hold values from 0.1 to 1.9
- vision_fc1: bfloat16 [1280, 5120], P(None, 'tp'), may hold values from -0.15625 to 0.15625
- vision_fc2: bfloat16 [5120, 1280], P('tp'), may hold values from -0.078125 to 0.078125
- vision_gate: float32 [1], replicated, may hold values from -2.5 to 2.5
- projector: bfloat16 [1280, 8192], P(None, 'tp'), may hold values from -0.15625 to 0.15625
- cross_norm: bfloat16 [2, 8192], P('section', 'tp'), may hold values from 0.099609375 to 1.8984375
- cross_q: bfloat16 [2, 8192, 4096], P('section', None, 'tp'), may hold values from -0.0625 to 0.0625
- cross_kv: bfloat16 [2, 8192, 1024], P('section', 'tp'), may hold values from -0.0625 to 0.0625
- cross_qk_gain: float32 [2, 2, 128], P('section'), may hold values from 0.1 to 1.9
- cross_o: bfloat16 [2, 4096, 8192], P('section', None, 'tp'), may hold values from -0.5 to 0.5
- cross_gate: float32 [2], P('section'), may hold values from 0.5 to 1.5
- self_norm: bfloat16 [2, 8192], P('section', 'tp'), may hold values from 0.5 to 1.5
- self_q: bfloat16 [2, 8192, 4096], P('section', None, 'tp'), may hold values from -1 to 1
- self_kv: bfloat16 [2, 8192, 1024], P('section', 'tp'), may hold values from -1 to 1
- self_o: bfloat16 [2, 4096, 8192], P('section', None, 'tp'), may hold values from -0.09375 to 0.09375
Outputs:
- section_outputs: bfloat16 [2, 128, 8192], P('section', None, 'tp')
The draws below stay inside these ranges and needn't reach their ends.
All inputs are finite; a program needn't handle non-finite values.
Results may differ from the reference program's by a relative error of at most 0.018.
Values may be sent and summed in bfloat16 or wider, within the bound.
No kernel may reach another device: no remote copies, remote signals or barrier semaphores. Data moves between devices by JAX's collectives and lax.ppermute only.
A program may use at most 128 MiB of HBM per device.

```python
import jax
import jax.numpy as jnp
from jax import lax

D = 8192
VW = 1280
VFF = 5120
HD = 128
HEADS = 32
KV = 4
TILES = 4
SEQ = 128
IMG = 256
SECTIONS = 2


def draw_text_states(key, part):
    key = jax.random.fold_in(key, 11)
    key_base = jax.random.fold_in(key, 0)
    states = jax.random.truncated_normal(key_base, -6.0, 6.0, (SEQ, D), jnp.float32)
    return states.astype(jnp.bfloat16)


def draw_self_q(key, part):
    key = jax.random.fold_in(key, 12)
    weights = jax.random.truncated_normal(key, -6.0, 6.0, (SECTIONS, D, HEADS * HD), jnp.float32) * D ** (-0.5)
    return weights.astype(jnp.bfloat16)


def draw_self_kv(key, part):
    key = jax.random.fold_in(key, 13)
    weights = jax.random.truncated_normal(key, -6.0, 6.0, (SECTIONS, D, 2 * KV * HD), jnp.float32) * D ** (-0.5)
    return weights.astype(jnp.bfloat16)


def set_ends(array, stream_key, smallest, largest):
    index_at = [jax.random.randint(jax.random.fold_in(stream_key, axis), (), 0, length) for axis, length in enumerate(array.shape)]
    main_axis = array.shape.index(max(array.shape))
    next_to = index_at[:main_axis] + [(index_at[main_axis] + 1) % array.shape[main_axis]] + index_at[main_axis + 1:]
    return array.at[tuple(index_at)].set(smallest).at[tuple(next_to)].set(largest)


def block_scale(rng, dims, shards, smallest, top_value):
    def one(dim, parts):
        steps = jax.random.uniform(jax.random.fold_in(jax.random.fold_in(rng, 6), dim), (parts,), jnp.float32, smallest / len(shards), top_value / len(shards))
        return jnp.repeat(jnp.exp(steps), dims[dim] // parts).reshape((-1,) + (1,) * (len(dims) - dim - 1))

    gain = one(*shards[0])
    for cut in shards[1:]:
        gain = gain * one(*cut)
    return gain


def gaussian(stream_key, extent, scale, limit, cuts=(), kind=jnp.bfloat16):
    loudness = block_scale(stream_key, extent, cuts, -0.22, 0.18) if cuts else 1.0
    entries = jax.random.normal(stream_key, extent, jnp.float32) * scale * loudness
    return jnp.minimum(jnp.maximum(entries, -limit), limit).astype(kind)


def setup_inputs(seed: int = 0) -> dict:
    keys = jax.random.split(jax.random.key(seed), 19)
    text_states = draw_text_states(jax.random.fold_in(keys[18], 71), 0)
    vision_states = gaussian(keys[1], (IMG, VW), 1.0, 6.0, ((0, 2),))
    visible_tiles = set_ends(jax.random.randint(keys[2], (SEQ,), 0, 5), jax.random.fold_in(keys[2], 1), 0, 4).astype(jnp.int32)
    vision_norm_gain = jnp.clip(1.0 + 0.18 * jax.random.normal(keys[3], (VW,), jnp.float32), 0.1, 1.9)
    vision_fc1 = gaussian(keys[4], (VW, VFF), VW ** -0.5, 0.15625, ((1, 16),))
    vision_fc2 = gaussian(keys[5], (VFF, VW), VFF ** -0.5, 0.078125, ((0, 16),))
    vision_gate = jnp.clip(jax.random.uniform(keys[6], (1,), jnp.float32, -2.5, 2.5), -2.5, 2.5)
    projector = gaussian(keys[7], (VW, D), VW ** -0.5, 0.15625, ((1, 16),))
    cross_norm = jnp.clip(1.0 + 0.18 * jax.random.normal(keys[8], (SECTIONS, D), jnp.float32), 0.099609375, 1.8984375).astype(jnp.bfloat16)
    cross_q = gaussian(keys[9], (SECTIONS, D, HEADS * HD), D ** -0.5, 0.0625, ((0, 2), (2, 16)))
    cross_kv = gaussian(keys[10], (SECTIONS, D, 2 * KV * HD), D ** -0.5, 0.0625, ((0, 2), (1, 16)))
    cross_qk_gain = jnp.clip(1.0 + 0.18 * jax.random.normal(keys[11], (SECTIONS, 2, HD), jnp.float32), 0.1, 1.9)
    cross_o = gaussian(keys[12], (SECTIONS, HEADS * HD, D), HD ** -0.5, 0.5, ((0, 2), (2, 16)))
    cross_gate = jnp.clip(0.5 + 1.0 * jax.random.uniform(keys[13], (SECTIONS,), jnp.float32) ** block_scale(keys[13], (SECTIONS,), ((0, 2),), -0.2, 0.2), 0.5, 1.5)
    self_norm = jnp.clip(1.0 + 0.1 * jax.random.normal(keys[14], (SECTIONS, D), jnp.float32), 0.5, 1.5).astype(jnp.bfloat16)
    self_q = draw_self_q(jax.random.fold_in(keys[18], 71), 0)
    self_kv = draw_self_kv(jax.random.fold_in(keys[18], 71), 0)
    self_o = gaussian(keys[17], (SECTIONS, HEADS * HD, D), (HEADS * HD) ** -0.5, 0.09375, ((0, 2), (2, 16)))
    return dict(text_states=text_states, vision_states=vision_states, visible_tiles=visible_tiles, vision_norm_gain=vision_norm_gain, vision_fc1=vision_fc1, vision_fc2=vision_fc2, vision_gate=vision_gate, projector=projector, cross_norm=cross_norm, cross_q=cross_q, cross_kv=cross_kv, cross_qk_gain=cross_qk_gain, cross_o=cross_o, cross_gate=cross_gate, self_norm=self_norm, self_q=self_q, self_kv=self_kv, self_o=self_o)


epsilon = 1e-05

def rms_norm(values, gain_row):
    mean_square = lax.optimization_barrier(jnp.mean(values * values, axis=-1, keepdims=True))
    return values * lax.rsqrt(mean_square + epsilon) * gain_row.astype(jnp.float32)

def rotate(values, positions):
    half_dim = values.shape[-1] // 2
    exponents = jnp.arange(half_dim, dtype=jnp.float32) * (2.0 / values.shape[-1])
    inverse = jnp.float32(500000.0) ** (-exponents)
    angles = positions.astype(jnp.float32)[:, None] * inverse[None, :]
    cosine = jnp.cos(angles)[:, None, :]
    sine = jnp.sin(angles)[:, None, :]
    lower = values[..., :half_dim]
    upper = values[..., half_dim:]
    return jnp.concatenate([lower * cosine - upper * sine, upper * cosine + lower * sine], axis=-1)

def softmax_rows(scores):
    top_score = lax.optimization_barrier(jnp.max(scores, axis=-1, keepdims=True))
    raised = jnp.exp(scores - top_score)
    return raised / lax.optimization_barrier(jnp.sum(raised, axis=-1, keepdims=True))

def attend(queries, key_rows, value_rows, allowed):
    row_count = queries.shape[0]
    kv_group = HEADS // KV
    grouped = queries.astype(jnp.float32).reshape(row_count, KV, kv_group, HD)
    scores = jnp.einsum('rkgd,jkd->kgrj', grouped, key_rows.astype(jnp.float32)) * HD ** (-0.5)
    scores = jnp.where(allowed[None, None], scores, -1e+30)
    weights = softmax_rows(scores).astype(jnp.bfloat16)
    mixed_heads = jnp.einsum('kgrj,jkd->rkgd', weights.astype(jnp.float32), value_rows.astype(jnp.float32))
    return mixed_heads.astype(jnp.bfloat16).reshape(row_count, HEADS * HD)

def reference(text_states, vision_states, visible_tiles, vision_norm_gain, vision_fc1, vision_fc2, vision_gate, projector, cross_norm, cross_q, cross_kv, cross_qk_gain, cross_o, cross_gate, self_norm, self_q, self_kv, self_o):
    vis_f32 = vision_states.astype(jnp.float32)
    centre = lax.optimization_barrier(jnp.mean(vis_f32, axis=-1, keepdims=True))
    spread = lax.optimization_barrier(jnp.mean((vis_f32 - centre) ** 2, axis=-1, keepdims=True))
    normed_vis = ((vis_f32 - centre) * lax.rsqrt(spread + epsilon) * vision_norm_gain.astype(jnp.float32)).astype(jnp.bfloat16)
    vis_hidden = jax.nn.gelu(jnp.dot(normed_vis, vision_fc1, preferred_element_type=jnp.float32), approximate=False).astype(jnp.bfloat16)
    vis_branch = jnp.dot(vis_hidden, vision_fc2, preferred_element_type=jnp.float32)
    vis_out = (vis_f32 + jnp.tanh(vision_gate[0]) * vis_branch).astype(jnp.bfloat16)
    image_feats = jnp.dot(vis_out, projector, preferred_element_type=jnp.float32).astype(jnp.bfloat16)
    image_count = image_feats.shape[0]
    row_tiles = visible_tiles
    tile_of = jnp.arange(image_count, dtype=jnp.int32) // (image_count // TILES)
    allowed = tile_of[None, :] < row_tiles[:, None]
    row_live = (row_tiles > 0).astype(jnp.float32)[:, None]
    seq_len = text_states.shape[0]
    positions = jnp.arange(seq_len, dtype=jnp.int32)
    causal = positions[None, :] <= positions[:, None]
    hidden = text_states
    results = []
    for section_no in range(SECTIONS):
        kv_image = jnp.dot(image_feats, cross_kv[section_no], preferred_element_type=jnp.float32)
        key_img = rms_norm(kv_image[:, :KV * HD].reshape(image_count, KV, HD), cross_qk_gain[section_no, 1]).astype(jnp.bfloat16)
        val_img = kv_image[:, KV * HD:].reshape(image_count, KV, HD).astype(jnp.bfloat16)
        normed = rms_norm(hidden.astype(jnp.float32), cross_norm[section_no]).astype(jnp.bfloat16)
        queries = jnp.dot(normed, cross_q[section_no], preferred_element_type=jnp.float32).reshape(seq_len, HEADS, HD)
        queries = rms_norm(queries, cross_qk_gain[section_no, 0]).astype(jnp.bfloat16)
        mixed = attend(queries, key_img, val_img, allowed)
        cross_branch = jnp.dot(mixed, cross_o[section_no], preferred_element_type=jnp.float32) * row_live
        hidden = (hidden.astype(jnp.float32) + jnp.tanh(cross_gate[section_no]) * cross_branch).astype(jnp.bfloat16)
        normed = rms_norm(hidden.astype(jnp.float32), self_norm[section_no]).astype(jnp.bfloat16)
        queries = rotate(jnp.dot(normed, self_q[section_no], preferred_element_type=jnp.float32).reshape(seq_len, HEADS, HD), positions).astype(jnp.bfloat16)
        kv_text = jnp.dot(normed, self_kv[section_no], preferred_element_type=jnp.float32)
        key_text = rotate(kv_text[:, :KV * HD].reshape(seq_len, KV, HD), positions).astype(jnp.bfloat16)
        val_text = kv_text[:, KV * HD:].reshape(seq_len, KV, HD).astype(jnp.bfloat16)
        mixed = attend(queries, key_text, val_text, causal)
        hidden = (hidden.astype(jnp.float32) + jnp.dot(mixed, self_o[section_no], preferred_element_type=jnp.float32)).astype(jnp.bfloat16)
        results.append(hidden)
    return jnp.stack(results)
```

```python
import functools

import jax
import jax.numpy as jnp
from jax import lax
from jax.experimental import pallas as pl
from jax.experimental.pallas import tpu as pltpu
from jax.sharding import PartitionSpec as P

HD = 128
HEADS = 32
KV = 4
TILES = 4
ROWS = 64
BLOCKS = 2


epsilon = 1e-05


def from_behind(block, axis, distance):
    devices = range(lax.axis_size(axis))
    route = [(i - distance, i) for i in devices if i - distance in devices]
    return lax.ppermute(block, axis, route)


def rms_norm(values, gain_row):
    mean_square = jnp.mean(values * values, axis=-1, keepdims=True)
    return values * lax.rsqrt(mean_square + epsilon) * gain_row.astype(jnp.float32)


def rotate(values, positions):
    half_dim = values.shape[-1] // 2
    exponents = jnp.arange(half_dim, dtype=jnp.float32) * (2.0 / values.shape[-1])
    inverse = jnp.float32(500000.0) ** (-exponents)
    angles = positions.astype(jnp.float32)[:, None] * inverse[None, :]
    cosine = jnp.cos(angles)[:, None, :]
    sine = jnp.sin(angles)[:, None, :]
    lower = values[..., :half_dim]
    upper = values[..., half_dim:]
    return jnp.concatenate([lower * cosine - upper * sine, upper * cosine + lower * sine], axis=-1)


def softmax_rows(scores):
    top_score = jnp.max(scores, axis=-1, keepdims=True)
    raised = jnp.exp(scores - top_score)
    return raised / jnp.sum(raised, axis=-1, keepdims=True)


def head_columns(kv_rows, kv_head):
    key_part = lax.dynamic_slice_in_dim(kv_rows, kv_head * HD, HD, 1)
    value_part = lax.dynamic_slice_in_dim(kv_rows, (KV + kv_head) * HD, HD, 1)
    return (key_part, value_part)


def attend_one(queries, key_rows, value_rows, allowed):
    scores = jnp.einsum(
        "rhd,jd->hrj", queries, key_rows, preferred_element_type=jnp.float32
    ) * HD ** (-0.5)
    scores = jnp.where(allowed[None], scores, -1e30)
    weights = softmax_rows(scores).astype(jnp.bfloat16)
    mixed_heads = jnp.einsum("hrj,jd->rhd", weights, value_rows, preferred_element_type=jnp.float32)
    return mixed_heads.astype(jnp.bfloat16).reshape(queries.shape[0], -1)


def out_fold(weight, segment):
    return jnp.dot(segment, weight, preferred_element_type=jnp.float32)


def blocked_body(
    text_states,
    vision_states,
    visible_tiles,
    vision_norm_gain,
    vision_fc1,
    vision_fc2,
    vision_gate,
    projector,
    cross_norm,
    cross_q,
    cross_kv,
    cross_qk_gain,
    cross_o,
    cross_gate,
    self_norm,
    self_q,
    self_kv,
    self_o,
):
    section_idx = lax.axis_index("section")
    section_total = lax.axis_size("section")
    tp_index = lax.axis_index("tp")
    local_width = text_states.shape[1]
    heads_local = cross_q.shape[2] // HD
    kv_group = HEADS // KV
    kv_head = tp_index * heads_local // kv_group
    vis_f32 = vision_states.astype(jnp.float32)
    centre = jnp.mean(vis_f32, axis=-1, keepdims=True)
    spread = jnp.mean((vis_f32 - centre) ** 2, axis=-1, keepdims=True)
    normed_vis = ((vis_f32 - centre) * lax.rsqrt(spread + epsilon) * vision_norm_gain).astype(
        jnp.bfloat16
    )
    vis_hidden = jax.nn.gelu(
        jnp.dot(normed_vis, vision_fc1, preferred_element_type=jnp.float32), approximate=False
    ).astype(jnp.bfloat16)
    vis_branch = lax.psum(jnp.dot(vis_hidden, vision_fc2, preferred_element_type=jnp.float32), "tp")
    vis_out = (vis_f32 + jnp.tanh(vision_gate[0]) * vis_branch).astype(jnp.bfloat16)
    every_row = lax.all_gather(vis_out, "section", axis=0, tiled=True)
    image_feats = jnp.dot(every_row, projector, preferred_element_type=jnp.float32).astype(
        jnp.bfloat16
    )
    image_count = image_feats.shape[0]
    kv_term = jnp.dot(image_feats, cross_kv[0], preferred_element_type=jnp.float32)
    key_gain = cross_qk_gain[0, 1]
    kv_image = lax.psum(kv_term, "tp")
    key_part, value_part = head_columns(kv_image, kv_head)
    key_img = rms_norm(key_part, key_gain).astype(jnp.bfloat16)
    val_img = value_part.astype(jnp.bfloat16)
    tile_of = jnp.arange(image_count, dtype=jnp.int32) // (image_count // TILES)
    seq_len = text_states.shape[0]
    positions_all = jnp.arange(seq_len, dtype=jnp.int32)
    gate_cross = jnp.tanh(cross_gate[0])
    key_cache = jnp.zeros((seq_len, HD), jnp.bfloat16)
    val_cache = jnp.zeros((seq_len, HD), jnp.bfloat16)
    outputs = jnp.zeros((seq_len, local_width), jnp.bfloat16)
    incoming = jnp.zeros((ROWS, local_width), jnp.bfloat16)
    step_count = BLOCKS + section_total - 1
    for step_no in range(step_count):
        block_idx = step_no - section_idx
        is_live = (block_idx >= 0) & (block_idx < BLOCKS)
        row_start = jnp.clip(block_idx, 0, BLOCKS - 1) * ROWS
        entry_block = min(step_no, BLOCKS - 1)
        first_rows = text_states[entry_block * ROWS : (entry_block + 1) * ROWS]
        current = jnp.where(section_idx == 0, first_rows, incoming)
        positions = row_start + jnp.arange(ROWS, dtype=jnp.int32)
        whole_rows, gain_row = (
            lax.all_gather(current, "tp", axis=1, tiled=True),
            lax.all_gather(cross_norm, "tp", axis=1, tiled=True),
        )
        normed = rms_norm(whole_rows.astype(jnp.float32), gain_row[0]).astype(jnp.bfloat16)
        queries = jnp.dot(normed, cross_q[0], preferred_element_type=jnp.float32).reshape(
            ROWS, heads_local, HD
        )
        queries = rms_norm(queries, cross_qk_gain[0, 0]).astype(jnp.bfloat16)
        row_tiles = lax.dynamic_slice_in_dim(visible_tiles, row_start, ROWS)
        allowed = tile_of[None, :] < row_tiles[:, None]
        mixed_heads = attend_one(queries, key_img, val_img, allowed)
        cross_branch = out_fold(cross_o[0], lax.all_gather(mixed_heads, "tp", axis=1, tiled=True))
        cross_branch = cross_branch * (row_tiles > 0).astype(jnp.float32)[:, None]
        current = (current.astype(jnp.float32) + gate_cross * cross_branch).astype(jnp.bfloat16)
        whole_rows, gain_row = (
            lax.all_gather(current, "tp", axis=1, tiled=True),
            lax.all_gather(self_norm, "tp", axis=1, tiled=True),
        )
        normed = rms_norm(whole_rows.astype(jnp.float32), gain_row[0]).astype(jnp.bfloat16)
        queries = rotate(
            jnp.dot(normed, self_q[0], preferred_element_type=jnp.float32).reshape(
                ROWS, heads_local, HD
            ),
            positions,
        ).astype(jnp.bfloat16)
        own_cols = lax.dynamic_slice_in_dim(normed, tp_index * local_width, local_width, 1)
        kv_text = lax.psum(
            jnp.dot(own_cols, self_kv[0], preferred_element_type=jnp.float32).astype(jnp.bfloat16),
            "tp",
        ).astype(jnp.float32)
        key_part, value_part = head_columns(kv_text, kv_head)
        new_keys = rotate(key_part[:, None, :], positions)[:, 0].astype(jnp.bfloat16)
        new_vals = value_part.astype(jnp.bfloat16)
        key_cache = jnp.where(
            is_live, lax.dynamic_update_slice_in_dim(key_cache, new_keys, row_start, 0), key_cache
        )
        val_cache = jnp.where(
            is_live, lax.dynamic_update_slice_in_dim(val_cache, new_vals, row_start, 0), val_cache
        )
        causal = positions_all[None, :] <= positions[:, None]
        mixed_heads = attend_one(queries, key_cache, val_cache, causal)
        self_branch = out_fold(self_o[0], lax.all_gather(mixed_heads, "tp", axis=1, tiled=True))
        current = (current.astype(jnp.float32) + self_branch).astype(jnp.bfloat16)
        outputs = jnp.where(
            is_live, lax.dynamic_update_slice_in_dim(outputs, current, row_start, 0), outputs
        )
        if step_no + 1 < step_count:
            incoming = from_behind(current, "section", 1)
    return outputs[None]


VMEM_LIMIT = 48 * 1024 * 1024
GROUP = 4


def params():
    return pltpu.CompilerParams(vmem_limit_bytes=VMEM_LIMIT)


def in_vmem():
    return pl.BlockSpec(memory_space=pltpu.VMEM)


def in_place():
    return pl.BlockSpec(memory_space=pl.ANY)


def swap_cores(block):
    return lax.ppermute(block, "section", [(0, 1), (1, 0)])


def send_xor(block, masks):
    chips = lax.axis_size("tp")
    route = [
        (core * chips + chip, core * chips + (chip ^ masks[core]))
        for core in range(2)
        for chip in range(chips)
    ]
    return lax.ppermute(block, ("section", "tp"), route)


def gather_chips(block):
    first = jnp.stack(
        [block] + [send_xor(block, (GROUP * k, k)) for k in range(1, GROUP)]
    )
    return [first] + [send_xor(first, (k, GROUP * k)) for k in range(1, GROUP)]


def piece_chip(core, chip, outer, inner):
    return jnp.where(core == 0, chip ^ (GROUP * inner) ^ outer, chip ^ inner ^ (GROUP * outer))


def fetch_rows(section, own_ref, other_ref, wbuf, sems, rows, columns):
    core = lax.axis_index("section")
    chip = lax.axis_index("tp")
    for outer in range(GROUP):
        for inner in range(GROUP):
            at = outer * GROUP + inner
            source = piece_chip(core, chip, outer, inner)
            start = pl.multiple_of(source * (2 * rows) + core * rows, rows)
            target = wbuf.at[at, :, pl.ds(0, columns)]

            @pl.when(core == section)
            def _():
                pltpu.make_async_copy(own_ref.at[pl.ds(start, rows), :], target, sems.at[at]).start()

            @pl.when(core != section)
            def _():
                pltpu.make_async_copy(other_ref.at[pl.ds(start, rows), :], target, sems.at[at]).start()


def wait_rows(own_ref, wbuf, sems, at, rows, columns):
    pltpu.make_async_copy(
        own_ref.at[pl.ds(0, rows), :], wbuf.at[at, :, pl.ds(0, columns)], sems.at[at]
    ).wait()


def query_kernel(section, gain_at, with_kv, *refs):
    x_refs = refs[:GROUP]
    gain_ref, own_ref, other_ref = refs[GROUP : GROUP + 3]
    rest = refs[GROUP + 3 :]
    if with_kv:
        kv_refs, rest = rest[:GROUP], rest[GROUP:]
    keep_ref, send_ref, wbuf, sems = rest[:4]
    core = lax.axis_index("section")
    rows = x_refs[0].shape[2]
    queries = own_ref.shape[1]
    fetch_rows(section, own_ref, other_ref, wbuf, sems, rows, queries)
    if with_kv:
        kv_sems = rest[4]
        width = kv_refs[0].shape[3]
        for outer in range(GROUP):
            for inner in range(GROUP):
                at = outer * GROUP + inner
                target = wbuf.at[at, :, pl.ds(queries, width)]

                @pl.when(core == 0)
                def _():
                    pltpu.make_async_copy(
                        kv_refs[outer].at[inner, section], target, kv_sems.at[at]
                    ).start()

                @pl.when(core != 0)
                def _():
                    pltpu.make_async_copy(
                        kv_refs[inner].at[outer, section], target, kv_sems.at[at]
                    ).start()

    total = jnp.zeros((x_refs[0].shape[1], wbuf.shape[2]), jnp.float32)
    squares = jnp.zeros(x_refs[0].shape[1:], jnp.float32)
    for outer in range(GROUP):
        for inner in range(GROUP):
            at = outer * GROUP + inner
            piece = x_refs[outer][inner].astype(jnp.float32)
            squares = squares + piece * piece
            gain_row = gain_ref[at, gain_at : gain_at + 1, :].astype(jnp.float32)
            scaled = (piece * gain_row).astype(jnp.bfloat16)
            wait_rows(own_ref, wbuf, sems, at, rows, queries)
            if with_kv:
                pltpu.make_async_copy(
                    kv_refs[0].at[0, section], wbuf.at[at, :, pl.ds(queries, width)], kv_sems.at[at]
                ).wait()
            total = total + jnp.dot(scaled, wbuf[at], preferred_element_type=jnp.float32)
    half = queries // 2
    lower, upper = total[:, :half], total[:, half:queries]
    keep_ref[:, :half] = jnp.where(core == 0, lower, upper)
    send_ref[:, :half] = jnp.where(core == 0, upper, lower)
    square_sum = jnp.broadcast_to(
        jnp.sum(squares, axis=1, keepdims=True), (squares.shape[0], 128)
    )
    for ref in (keep_ref, send_ref):
        ref[:, half : half + 128] = square_sum
        if with_kv:
            ref[:, half + 128 :] = total[:, queries:]


def query_part(section, gain_at, pieces, gains, own, other, kv_pieces=None):
    rows = pieces[0].shape[1]
    depth = pieces[0].shape[2]
    queries = own.shape[1]
    kv_width = kv_pieces[0].shape[3] if kv_pieces is not None else 0
    out = jax.ShapeDtypeStruct((rows, queries // 2 + 128 + kv_width), jnp.float32)
    scratch = [
        pltpu.VMEM((GROUP * GROUP, depth, queries + kv_width), jnp.bfloat16),
        pltpu.SemaphoreType.DMA((GROUP * GROUP,)),
    ]
    operands = list(pieces) + [gains, own, other]
    specs = [in_vmem()] * (GROUP + 1) + [in_place()] * 2
    if kv_pieces is not None:
        scratch.append(pltpu.SemaphoreType.DMA((GROUP * GROUP,)))
        operands += list(kv_pieces)
        specs += [in_place()] * GROUP
    return pl.pallas_call(
        functools.partial(query_kernel, section, gain_at, kv_pieces is not None),
        out_shape=(out, out),
        in_specs=specs,
        out_specs=(in_vmem(), in_vmem()),
        scratch_shapes=scratch,
        compiler_params=params(),
    )(*operands)


def out_kernel(section, *refs):
    x_refs = refs[:GROUP]
    own_ref, other_ref, keep_ref, send_ref, wbuf, sems = refs[GROUP:]
    core = lax.axis_index("section")
    rows = x_refs[0].shape[2]
    columns = own_ref.shape[1]
    fetch_rows(section, own_ref, other_ref, wbuf, sems, rows, columns)
    total = jnp.zeros((x_refs[0].shape[1], columns), jnp.float32)
    for outer in range(GROUP):
        for inner in range(GROUP):
            at = outer * GROUP + inner
            wait_rows(own_ref, wbuf, sems, at, rows, columns)
            total = total + jnp.dot(
                x_refs[outer][inner], wbuf[at], preferred_element_type=jnp.float32
            )
    half = columns // 2
    lower, upper = total[:, :half], total[:, half:]
    keep_ref[...] = jnp.where(core == 0, lower, upper)
    send_ref[...] = jnp.where(core == 0, upper, lower)


def out_part(section, pieces, own, other):
    rows, depth = pieces[0].shape[1:]
    columns = own.shape[1]
    out = jax.ShapeDtypeStruct((rows, columns // 2), jnp.float32)
    return pl.pallas_call(
        functools.partial(out_kernel, section),
        out_shape=(out, out),
        in_specs=[in_vmem()] * GROUP + [in_place()] * 2,
        out_specs=(in_vmem(), in_vmem()),
        scratch_shapes=[
            pltpu.VMEM((GROUP * GROUP, depth, columns), jnp.bfloat16),
            pltpu.SemaphoreType.DMA((GROUP * GROUP,)),
        ],
        compiler_params=params(),
    )(*pieces, own, other)


def dot_rows(left, right):
    return lax.dot_general(
        left, right, (((1,), (1,)), ((), ())), preferred_element_type=jnp.float32
    )


def row_scale(keep_ref, come_ref, width):
    square_sum = keep_ref[:, HD : HD + 128] + come_ref[:, HD : HD + 128]
    return lax.rsqrt(square_sum / width + epsilon)


def cross_kernel(width, tile_rows, keep_ref, come_ref, near_ref, far_ref, tiles_ref, gain_ref, out_ref):
    core = lax.axis_index("section")
    queries = (keep_ref[:, :HD] + come_ref[:, :HD]) * row_scale(keep_ref, come_ref, width)
    queries = rms_norm(queries, gain_ref[0:1, :]).astype(jnp.bfloat16)
    row_tiles = tiles_ref[...]
    count = near_ref.shape[0]
    key_at = lax.broadcasted_iota(jnp.int32, (queries.shape[0], count), 1)
    scores = []
    for ref, base in ((near_ref, core * count), (far_ref, (1 - core) * count)):
        part = dot_rows(queries, ref[:, :HD]) * HD ** (-0.5)
        scores.append(jnp.where(key_at + base < row_tiles * tile_rows, part, -1e30))
    top = jnp.maximum(
        jnp.max(scores[0], axis=1, keepdims=True), jnp.max(scores[1], axis=1, keepdims=True)
    )
    raised = [jnp.exp(part - top) for part in scores]
    bottom = jnp.sum(raised[0], axis=1, keepdims=True) + jnp.sum(raised[1], axis=1, keepdims=True)
    mixed = jnp.zeros(queries.shape, jnp.float32)
    for part, ref in zip(raised, (near_ref, far_ref)):
        weights = (part / bottom).astype(jnp.bfloat16)
        mixed = mixed + jnp.dot(weights, ref[:, HD:], preferred_element_type=jnp.float32)
    out_ref[...] = mixed.astype(jnp.bfloat16)


def cross_mix(width, tile_rows, keep, come, near, far, tiles, gain):
    return pl.pallas_call(
        functools.partial(cross_kernel, width, tile_rows),
        out_shape=jax.ShapeDtypeStruct((keep.shape[0], HD), jnp.bfloat16),
        in_specs=[in_vmem()] * 6,
        out_specs=in_vmem(),
        compiler_params=params(),
    )(keep, come, near, far, tiles, gain)


def turn(values, cosine, sine):
    half = HD // 2
    swapped = jnp.concatenate([values[:, half:], values[:, :half]], axis=1)
    return values * cosine + swapped * sine


def self_kernel(width, keep_ref, come_ref, cosine_ref, sine_ref, out_ref):
    scale = row_scale(keep_ref, come_ref, width)
    cosine, sine = cosine_ref[...], sine_ref[...]
    queries = (keep_ref[:, :HD] + come_ref[:, :HD]) * scale
    queries = turn(queries, cosine, sine).astype(jnp.bfloat16)
    at = HD + 128
    keys = (keep_ref[:, at : at + HD] + come_ref[:, at : at + HD]) * scale
    keys = turn(keys, cosine, sine).astype(jnp.bfloat16)
    values = (keep_ref[:, at + HD :] + come_ref[:, at + HD :]) * scale
    values = values.astype(jnp.bfloat16)
    scores = dot_rows(queries, keys) * HD ** (-0.5)
    row_at = lax.broadcasted_iota(jnp.int32, scores.shape, 0)
    key_at = lax.broadcasted_iota(jnp.int32, scores.shape, 1)
    scores = jnp.where(key_at <= row_at, scores, -1e30)
    weights = softmax_rows(scores).astype(jnp.bfloat16)
    mixed = jnp.dot(weights, values, preferred_element_type=jnp.float32)
    out_ref[...] = mixed.astype(jnp.bfloat16)


def self_mix(width, keep, come, cosine, sine):
    return pl.pallas_call(
        functools.partial(self_kernel, width),
        out_shape=jax.ShapeDtypeStruct((keep.shape[0], HD), jnp.bfloat16),
        in_specs=[in_vmem()] * 4,
        out_specs=in_vmem(),
        compiler_params=params(),
    )(keep, come, cosine, sine)


def image_kernel(p0, p1, p2, p3, projector_ref, own_ref, other_ref, out_ref, rows_ref, kv_ref):
    core = lax.axis_index("section")
    chip = lax.axis_index("tp")
    low, high = chip % GROUP, chip // GROUP
    member = jnp.where(core == 0, low, high)
    count = p0.shape[0]
    for k, ref in enumerate((p0, p1, p2, p3)):
        rows_ref[pl.ds(pl.multiple_of((member ^ k) * count, count), count), :] = ref[...]
    feats = jnp.dot(
        rows_ref[...], projector_ref[...], preferred_element_type=jnp.float32
    ).astype(jnp.bfloat16)
    for section in range(2):
        weight = jnp.where(core == section, own_ref[...], other_ref[...])
        kv_ref[...] = jnp.dot(feats, weight, preferred_element_type=jnp.float32)
        for k in range(GROUP):
            head = high ^ k
            for part in range(2):
                start = pl.multiple_of((part * KV + head) * HD, HD)
                out_ref[section, k, :, part * HD : (part + 1) * HD] = kv_ref[
                    :, pl.ds(start, HD)
                ].astype(jnp.bfloat16)


def image_part(pieces, projector, own, other):
    rows = GROUP * pieces[0].shape[0]
    return pl.pallas_call(
        image_kernel,
        out_shape=jax.ShapeDtypeStruct((2, GROUP, rows, 2 * HD), jnp.bfloat16),
        in_specs=[in_vmem()] * 7,
        out_specs=in_vmem(),
        scratch_shapes=[
            pltpu.VMEM((rows, projector.shape[0]), jnp.bfloat16),
            pltpu.VMEM((rows, own.shape[1]), jnp.float32),
        ],
        compiler_params=params(),
    )(*pieces, projector, own, other)


def heads_kernel(own_ref, other_ref, out_ref):
    core = lax.axis_index("section")
    high = lax.axis_index("tp") // GROUP
    rows = own_ref.shape[0] // 2
    mine = pl.ds(pl.multiple_of(core * rows, rows), rows)
    for k in range(GROUP):
        head = high ^ k
        for part in range(2):
            start = pl.multiple_of((part * KV + head) * HD, HD)
            near = own_ref[mine, pl.ds(start, HD)]
            far = other_ref[mine, pl.ds(start, HD)]
            columns = slice(part * HD, (part + 1) * HD)
            out_ref[k, 0, :, columns] = jnp.where(core == 0, near, far)
            out_ref[k, 1, :, columns] = jnp.where(core == 0, far, near)


def self_kv_pieces(own, other):
    rows = own.shape[0] // 2
    blocks = pl.pallas_call(
        heads_kernel,
        out_shape=jax.ShapeDtypeStruct((GROUP, 2, rows, 2 * HD), jnp.bfloat16),
        in_specs=[in_vmem()] * 2,
        out_specs=in_vmem(),
        compiler_params=params(),
    )(own, other)
    first = jnp.stack(
        [blocks[0]] + [send_xor(blocks[k], (GROUP * k, GROUP * k)) for k in range(1, GROUP)]
    )
    return [first] + [send_xor(first, (k, k)) for k in range(1, GROUP)]


def paired_body(
    text_states,
    vision_states,
    visible_tiles,
    vision_norm_gain,
    vision_fc1,
    vision_fc2,
    vision_gate,
    projector,
    cross_norm,
    cross_q,
    cross_kv,
    cross_qk_gain,
    cross_o,
    cross_gate,
    self_norm,
    self_q,
    self_kv,
    self_o,
):
    core = lax.axis_index("section")
    chip = lax.axis_index("tp")
    seq_len, local_width = text_states.shape
    half = local_width // 2
    full_width = local_width * lax.axis_size("tp")
    low, high = chip % GROUP, chip // GROUP
    member = jnp.where(core == 0, low, high)

    vis_f32 = vision_states.astype(jnp.float32)
    centre = jnp.mean(vis_f32, axis=-1, keepdims=True)
    spread = jnp.mean((vis_f32 - centre) ** 2, axis=-1, keepdims=True)
    normed_vis = ((vis_f32 - centre) * lax.rsqrt(spread + epsilon) * vision_norm_gain).astype(
        jnp.bfloat16
    )
    vis_hidden = jax.nn.gelu(
        jnp.dot(normed_vis, vision_fc1, preferred_element_type=jnp.float32), approximate=False
    ).astype(jnp.bfloat16)
    branch = jnp.dot(vis_hidden, vision_fc2, preferred_element_type=jnp.float32)
    rows = branch.shape[0] // GROUP
    branch = branch.astype(jnp.bfloat16).reshape(GROUP, rows, -1)

    def chunk(array, k):
        return lax.dynamic_index_in_dim(array, member ^ k, 0, keepdims=False)

    def total(parts):
        return sum((part.astype(jnp.float32) for part in parts[1:]), parts[0].astype(jnp.float32))

    near = total(
        [chunk(branch, 0)] + [send_xor(chunk(branch, k), (k, GROUP * k)) for k in range(1, GROUP)]
    ).astype(jnp.bfloat16)
    branch_rows = total([near] + [send_xor(near, (GROUP * k, k)) for k in range(1, GROUP)])
    vis_rows = chunk(vis_f32.reshape(GROUP, rows, -1), 0)
    vis_out = (vis_rows + jnp.tanh(vision_gate[0]) * branch_rows).astype(jnp.bfloat16)
    vis_pieces = [vis_out] + [send_xor(vis_out, (k, GROUP * k)) for k in range(1, GROUP)]

    small = jnp.concatenate(
        [
            cross_norm.astype(jnp.float32),
            self_norm.astype(jnp.float32),
            jnp.pad(cross_qk_gain.reshape(1, -1), ((0, 0), (0, local_width - 2 * HD))),
            jnp.broadcast_to(cross_gate[None], (1, local_width)),
        ]
    )
    small = lax.all_gather(small, "section", axis=0)
    own_cross_kv, own_cross_q, own_cross_o = cross_kv[0], cross_q[0], cross_o[0]
    own_self_kv, own_self_q, own_self_o = self_kv[0], self_q[0], self_o[0]
    far_cross_kv = swap_cores(own_cross_kv)
    far_cross_q = swap_cores(own_cross_q)
    far_self_kv = swap_cores(own_self_kv)
    far_cross_o = swap_cores(own_cross_o)
    far_self_q = swap_cores(own_self_q)
    far_self_o = swap_cores(own_self_o)

    gain_rows = small[:, :2].astype(jnp.bfloat16).reshape(4, local_width)
    entry = jnp.concatenate(
        [text_states, gain_rows, jnp.zeros((12, local_width), jnp.bfloat16)], axis=0
    )
    entry = lax.dynamic_slice_in_dim(entry, core * half, half, 1)
    hidden = entry[:seq_len]
    pieces = gather_chips(entry)
    gains = jnp.concatenate([piece[:, seq_len:] for piece in pieces], axis=0)
    pieces = [piece[:, :seq_len] for piece in pieces]

    image_parts = image_part(vis_pieces, projector, own_cross_kv, far_cross_kv)
    image_kv = []
    for section in range(2):
        near = total(
            [image_parts[section, 0]]
            + [
                send_xor(image_parts[section, k], (GROUP * k, GROUP * k))
                for k in range(1, GROUP)
            ]
        ).astype(jnp.bfloat16)
        kv_rows = total([near] + [send_xor(near, (k, k)) for k in range(1, GROUP)])
        key_gain = small[section, 2, HD : 2 * HD]
        near = jnp.concatenate(
            [rms_norm(kv_rows[:, :HD], key_gain), kv_rows[:, HD:]], axis=1
        ).astype(jnp.bfloat16)
        image_kv.append((near, swap_cores(near)))

    kv_pieces = self_kv_pieces(own_self_kv, far_self_kv)

    tile_rows = 2 * vision_states.shape[0] // TILES
    tiles = jnp.broadcast_to(visible_tiles[:, None], (seq_len, 128))
    row_live = (visible_tiles > 0).astype(jnp.float32)[:, None]
    exponents = jnp.arange(HD // 2, dtype=jnp.float32) * (2.0 / HD)
    inverse = jnp.float32(500000.0) ** (-exponents)
    angles = jnp.arange(seq_len, dtype=jnp.float32)[:, None] * inverse[None, :]
    cosine = jnp.tile(jnp.cos(angles), (1, 2))
    sine = jnp.concatenate([-jnp.sin(angles), jnp.sin(angles)], axis=1)

    results = []
    for section in range(2):
        if section > 0:
            pieces = gather_chips(hidden)
        keep, send = query_part(
            section, 2 * section, pieces, gains, own_cross_q, far_cross_q
        )
        near, far = image_kv[section]
        mixed = cross_mix(
            full_width, tile_rows, keep, swap_cores(send), near, far, tiles, small[section, 2:3, :HD]
        )
        keep, send = out_part(section, gather_chips(mixed), own_cross_o, far_cross_o)
        branch = (keep + swap_cores(send)) * row_live
        gate = jnp.tanh(small[section, 3, 0])
        hidden = (hidden.astype(jnp.float32) + gate * branch).astype(jnp.bfloat16)

        pieces = gather_chips(hidden)
        keep, send = query_part(
            section, 2 * section + 1, pieces, gains, own_self_q, far_self_q, kv_pieces
        )
        mixed = self_mix(full_width, keep, swap_cores(send), cosine, sine)
        keep, send = out_part(section, gather_chips(mixed), own_self_o, far_self_o)
        branch = keep + swap_cores(send)
        hidden = (hidden.astype(jnp.float32) + branch).astype(jnp.bfloat16)
        results.append(hidden)
    come = swap_cores(jnp.where(core == 0, results[1], results[0]))
    return jnp.where(
        core == 0,
        jnp.concatenate([results[0], come], axis=1),
        jnp.concatenate([come, results[1]], axis=1),
    )[None]


def solution(mesh):
    chips = mesh.shape["tp"]
    paired = mesh.shape["section"] == 2 and chips == GROUP * GROUP and HEADS == 2 * chips
    body = paired_body if paired else blocked_body
    in_specs = (
        P(None, "tp"),
        P("section", None),
        P(),
        P(),
        P(None, "tp"),
        P("tp", None),
        P(),
        P(None, "tp"),
        P("section", "tp"),
        P("section", None, "tp"),
        P("section", "tp", None),
        P("section", None, None),
        P("section", None, "tp"),
        P("section"),
        P("section", "tp"),
        P("section", None, "tp"),
        P("section", "tp", None),
        P("section", None, "tp"),
    )
    out_specs = P("section", None, "tp")
    return jax.shard_map(body, mesh=mesh, in_specs=in_specs, out_specs=out_specs, check_vma=False)
```

```python
import functools

import jax
import jax.numpy as jnp
import numpy as np
from jax import lax
from jax.experimental import pallas as pl
from jax.experimental.pallas import tpu as pltpu
from jax.sharding import PartitionSpec as P

HD = 128
HEADS = 32
KV = 4
TILES = 4
ROWS = 64
BLOCKS = 2


epsilon = 1e-05


def from_behind(block, axis, distance):
    devices = range(lax.axis_size(axis))
    route = [(i - distance, i) for i in devices if i - distance in devices]
    return lax.ppermute(block, axis, route)


def rms_norm(values, gain_row):
    mean_square = jnp.mean(values * values, axis=-1, keepdims=True)
    return values * lax.rsqrt(mean_square + epsilon) * gain_row.astype(jnp.float32)


def rotate(values, positions):
    half_dim = values.shape[-1] // 2
    exponents = jnp.arange(half_dim, dtype=jnp.float32) * (2.0 / values.shape[-1])
    inverse = jnp.float32(500000.0) ** (-exponents)
    angles = positions.astype(jnp.float32)[:, None] * inverse[None, :]
    cosine = jnp.cos(angles)[:, None, :]
    sine = jnp.sin(angles)[:, None, :]
    lower = values[..., :half_dim]
    upper = values[..., half_dim:]
    return jnp.concatenate([lower * cosine - upper * sine, upper * cosine + lower * sine], axis=-1)


def softmax_rows(scores):
    top_score = jnp.max(scores, axis=-1, keepdims=True)
    raised = jnp.exp(scores - top_score)
    return raised / jnp.sum(raised, axis=-1, keepdims=True)


def head_columns(kv_rows, kv_head):
    key_part = lax.dynamic_slice_in_dim(kv_rows, kv_head * HD, HD, 1)
    value_part = lax.dynamic_slice_in_dim(kv_rows, (KV + kv_head) * HD, HD, 1)
    return (key_part, value_part)


def attend_one(queries, key_rows, value_rows, allowed):
    scores = jnp.einsum(
        "rhd,jd->hrj", queries, key_rows, preferred_element_type=jnp.float32
    ) * HD ** (-0.5)
    scores = jnp.where(allowed[None], scores, -1e30)
    weights = softmax_rows(scores).astype(jnp.bfloat16)
    mixed_heads = jnp.einsum("hrj,jd->rhd", weights, value_rows, preferred_element_type=jnp.float32)
    return mixed_heads.astype(jnp.bfloat16).reshape(queries.shape[0], -1)


def out_fold(weight, segment):
    return jnp.dot(segment, weight, preferred_element_type=jnp.float32)


def blocked_body(
    text_states,
    vision_states,
    visible_tiles,
    vision_norm_gain,
    vision_fc1,
    vision_fc2,
    vision_gate,
    projector,
    cross_norm,
    cross_q,
    cross_kv,
    cross_qk_gain,
    cross_o,
    cross_gate,
    self_norm,
    self_q,
    self_kv,
    self_o,
):
    section_idx = lax.axis_index("section")
    section_total = lax.axis_size("section")
    tp_index = lax.axis_index("tp")
    local_width = text_states.shape[1]
    heads_local = cross_q.shape[2] // HD
    kv_group = HEADS // KV
    kv_head = tp_index * heads_local // kv_group
    vis_f32 = vision_states.astype(jnp.float32)
    centre = jnp.mean(vis_f32, axis=-1, keepdims=True)
    spread = jnp.mean((vis_f32 - centre) ** 2, axis=-1, keepdims=True)
    normed_vis = ((vis_f32 - centre) * lax.rsqrt(spread + epsilon) * vision_norm_gain).astype(
        jnp.bfloat16
    )
    vis_hidden = jax.nn.gelu(
        jnp.dot(normed_vis, vision_fc1, preferred_element_type=jnp.float32), approximate=False
    ).astype(jnp.bfloat16)
    vis_branch = lax.psum(jnp.dot(vis_hidden, vision_fc2, preferred_element_type=jnp.float32), "tp")
    vis_out = (vis_f32 + jnp.tanh(vision_gate[0]) * vis_branch).astype(jnp.bfloat16)
    every_row = lax.all_gather(vis_out, "section", axis=0, tiled=True)
    image_feats = jnp.dot(every_row, projector, preferred_element_type=jnp.float32).astype(
        jnp.bfloat16
    )
    image_count = image_feats.shape[0]
    kv_term = jnp.dot(image_feats, cross_kv[0], preferred_element_type=jnp.float32)
    key_gain = cross_qk_gain[0, 1]
    kv_image = lax.psum(kv_term, "tp")
    key_part, value_part = head_columns(kv_image, kv_head)
    key_img = rms_norm(key_part, key_gain).astype(jnp.bfloat16)
    val_img = value_part.astype(jnp.bfloat16)
    tile_of = jnp.arange(image_count, dtype=jnp.int32) // (image_count // TILES)
    seq_len = text_states.shape[0]
    positions_all = jnp.arange(seq_len, dtype=jnp.int32)
    gate_cross = jnp.tanh(cross_gate[0])
    key_cache = jnp.zeros((seq_len, HD), jnp.bfloat16)
    val_cache = jnp.zeros((seq_len, HD), jnp.bfloat16)
    outputs = jnp.zeros((seq_len, local_width), jnp.bfloat16)
    incoming = jnp.zeros((ROWS, local_width), jnp.bfloat16)
    step_count = BLOCKS + section_total - 1
    for step_no in range(step_count):
        block_idx = step_no - section_idx
        is_live = (block_idx >= 0) & (block_idx < BLOCKS)
        row_start = jnp.clip(block_idx, 0, BLOCKS - 1) * ROWS
        entry_block = min(step_no, BLOCKS - 1)
        first_rows = text_states[entry_block * ROWS : (entry_block + 1) * ROWS]
        current = jnp.where(section_idx == 0, first_rows, incoming)
        positions = row_start + jnp.arange(ROWS, dtype=jnp.int32)
        whole_rows, gain_row = (
            lax.all_gather(current, "tp", axis=1, tiled=True),
            lax.all_gather(cross_norm, "tp", axis=1, tiled=True),
        )
        normed = rms_norm(whole_rows.astype(jnp.float32), gain_row[0]).astype(jnp.bfloat16)
        queries = jnp.dot(normed, cross_q[0], preferred_element_type=jnp.float32).reshape(
            ROWS, heads_local, HD
        )
        queries = rms_norm(queries, cross_qk_gain[0, 0]).astype(jnp.bfloat16)
        row_tiles = lax.dynamic_slice_in_dim(visible_tiles, row_start, ROWS)
        allowed = tile_of[None, :] < row_tiles[:, None]
        mixed_heads = attend_one(queries, key_img, val_img, allowed)
        cross_branch = out_fold(cross_o[0], lax.all_gather(mixed_heads, "tp", axis=1, tiled=True))
        cross_branch = cross_branch * (row_tiles > 0).astype(jnp.float32)[:, None]
        current = (current.astype(jnp.float32) + gate_cross * cross_branch).astype(jnp.bfloat16)
        whole_rows, gain_row = (
            lax.all_gather(current, "tp", axis=1, tiled=True),
            lax.all_gather(self_norm, "tp", axis=1, tiled=True),
        )
        normed = rms_norm(whole_rows.astype(jnp.float32), gain_row[0]).astype(jnp.bfloat16)
        queries = rotate(
            jnp.dot(normed, self_q[0], preferred_element_type=jnp.float32).reshape(
                ROWS, heads_local, HD
            ),
            positions,
        ).astype(jnp.bfloat16)
        own_cols = lax.dynamic_slice_in_dim(normed, tp_index * local_width, local_width, 1)
        kv_text = lax.psum(
            jnp.dot(own_cols, self_kv[0], preferred_element_type=jnp.float32).astype(jnp.bfloat16),
            "tp",
        ).astype(jnp.float32)
        key_part, value_part = head_columns(kv_text, kv_head)
        new_keys = rotate(key_part[:, None, :], positions)[:, 0].astype(jnp.bfloat16)
        new_vals = value_part.astype(jnp.bfloat16)
        key_cache = jnp.where(
            is_live, lax.dynamic_update_slice_in_dim(key_cache, new_keys, row_start, 0), key_cache
        )
        val_cache = jnp.where(
            is_live, lax.dynamic_update_slice_in_dim(val_cache, new_vals, row_start, 0), val_cache
        )
        causal = positions_all[None, :] <= positions[:, None]
        mixed_heads = attend_one(queries, key_cache, val_cache, causal)
        self_branch = out_fold(self_o[0], lax.all_gather(mixed_heads, "tp", axis=1, tiled=True))
        current = (current.astype(jnp.float32) + self_branch).astype(jnp.bfloat16)
        outputs = jnp.where(
            is_live, lax.dynamic_update_slice_in_dim(outputs, current, row_start, 0), outputs
        )
        if step_no + 1 < step_count:
            incoming = from_behind(current, "section", 1)
    return outputs[None]


VMEM_LIMIT = 8 * 1024 * 1024
GROUP = 4


def params():
    return pltpu.CompilerParams(vmem_limit_bytes=VMEM_LIMIT)


def in_vmem():
    return pl.BlockSpec(memory_space=pltpu.VMEM)


def swap_cores(block):
    return lax.ppermute(block, "section", [(0, 1), (1, 0)])


def send_xor(block, masks):
    chips = lax.axis_size("tp")
    route = [
        (core * chips + chip, core * chips + (chip ^ masks[core]))
        for core in range(2)
        for chip in range(chips)
    ]
    return lax.ppermute(block, ("section", "tp"), route)


def gather_chips(block):
    first = jnp.stack(
        [block] + [send_xor(block, (GROUP * k, k)) for k in range(1, GROUP)]
    )
    return [first] + [send_xor(first, (k, GROUP * k)) for k in range(1, GROUP)]


def total(parts):
    return sum((part.astype(jnp.float32) for part in parts[1:]), parts[0].astype(jnp.float32))


def reduce_heads(blocks):
    near = total(
        [blocks[0]] + [send_xor(blocks[k], (GROUP * k, GROUP * k)) for k in range(1, GROUP)]
    ).astype(jnp.bfloat16)
    return total([near] + [send_xor(near, (k, k)) for k in range(1, GROUP)])


def piece_chip(core, chip, outer, inner):
    return jnp.where(core == 0, chip ^ (GROUP * inner) ^ outer, chip ^ inner ^ (GROUP * outer))


def with_weight(section, own_ref, other_ref, run):
    core = lax.axis_index("section")

    @pl.when(core == section)
    def _():
        run(own_ref)

    @pl.when(core != section)
    def _():
        run(other_ref)


def weight_rows(weight_ref, at, rows):
    source = piece_chip(lax.axis_index("section"), lax.axis_index("tp"), at // GROUP, at % GROUP)
    return weight_ref[pl.ds(pl.multiple_of(source * rows, rows), rows), :]


def project(section, gain_at, rows, x_refs, gain_ref, own_ref, other_ref, product_ref):
    depth = x_refs[0].shape[2]

    def run(weight_ref):
        product = jnp.zeros(product_ref.shape, jnp.float32)
        squares = jnp.zeros((rows, depth), jnp.float32)
        for at in range(GROUP * GROUP):
            piece = x_refs[at // GROUP][at % GROUP, :rows, :].astype(jnp.float32)
            squares = squares + piece * piece
            gain_row = gain_ref[at, gain_at : gain_at + 1, :].astype(jnp.float32)
            scaled = (piece * gain_row).astype(jnp.bfloat16)
            product = product + jnp.dot(
                scaled, weight_rows(weight_ref, at, depth), preferred_element_type=jnp.float32
            )
        mean_square = jnp.sum(squares, axis=1, keepdims=True) / (GROUP * GROUP * depth)
        product_ref[...] = product * lax.rsqrt(mean_square + epsilon)

    with_weight(section, own_ref, other_ref, run)
    return product_ref[...]


def dot_rows(left, right):
    return lax.dot_general(
        left, right, (((1,), (1,)), ((), ())), preferred_element_type=jnp.float32
    )


def mix(queries, key_sets, value_sets, allowed_sets, value_scales):
    scores = []
    for keys, allowed, scale in zip(key_sets, allowed_sets, value_scales):
        part = dot_rows(queries, keys) * HD ** (-0.5)
        if scale is not None:
            part = part * scale
        scores.append(jnp.where(allowed, part, -1e30))
    top = functools.reduce(
        jnp.maximum, [jnp.max(part, axis=1, keepdims=True) for part in scores]
    )
    raised = [jnp.exp(part - top) for part in scores]
    bottom = sum(jnp.sum(part, axis=1, keepdims=True) for part in raised)
    mixed = jnp.zeros(queries.shape, jnp.float32)
    for part, values, scale in zip(raised, value_sets, value_scales):
        weights = part / bottom
        if scale is not None:
            weights = weights * scale
        mixed = mixed + jnp.dot(
            weights.astype(jnp.bfloat16), values, preferred_element_type=jnp.float32
        )
    return mixed.astype(jnp.bfloat16)


def by_head(queries):
    heads = queries.shape[1] // HD
    return jnp.concatenate([queries[:, h * HD : (h + 1) * HD] for h in range(heads)], axis=0)


def side_by_side(mixed, rows):
    return jnp.concatenate(
        [mixed[start : start + rows] for start in range(0, mixed.shape[0], rows)], axis=1
    )


def cross_attend(tile_rows, queries, near_ref, far_ref, tiles_ref, qk_ref, out_ref):
    core = lax.axis_index("section")
    rows = out_ref.shape[0]
    queries = rms_norm(by_head(queries), qk_ref[2:3, :HD]).astype(jnp.bfloat16)
    row_tiles = tiles_ref[pl.ds(pl.multiple_of(core * rows, rows), rows), :]
    row_tiles = jnp.concatenate([row_tiles] * (queries.shape[0] // rows), axis=0)
    count = near_ref.shape[0]
    key_at = lax.broadcasted_iota(jnp.int32, (queries.shape[0], count), 1)
    allowed = [
        key_at + core * count < row_tiles * tile_rows,
        key_at + (1 - core) * count < row_tiles * tile_rows,
    ]
    sets = (near_ref[...], far_ref[...])
    mixed = mix(
        queries, [kv[:, :HD] for kv in sets], [kv[:, HD:] for kv in sets], allowed, (None, None)
    )
    out_ref[...] = side_by_side(mixed, rows)


def cross_kernel(section, gain_at, tile_rows, *refs):
    x_refs = refs[:GROUP]
    (gain_ref, near_ref, far_ref, tiles_ref, qk_ref, own_ref, other_ref) = refs[GROUP : GROUP + 7]
    out_ref, product_ref = refs[GROUP + 7 :]
    rows = out_ref.shape[0]
    queries = project(section, gain_at, rows, x_refs, gain_ref, own_ref, other_ref, product_ref)
    cross_attend(tile_rows, queries, near_ref, far_ref, tiles_ref, qk_ref, out_ref)


def cross_mix(section, gain_at, tile_rows, rows, pieces, gains, near, far, tiles, qk, own, other):
    columns = own.shape[1]
    return pl.pallas_call(
        functools.partial(cross_kernel, section, gain_at, tile_rows),
        out_shape=jax.ShapeDtypeStruct((rows, columns), jnp.bfloat16),
        in_specs=[in_vmem()] * (GROUP + 7),
        out_specs=in_vmem(),
        scratch_shapes=[pltpu.VMEM((rows, columns), jnp.float32)],
        compiler_params=params(),
    )(*pieces, gains, near, far, tiles, qk, own, other)


def attend_kernel(tile_rows, q_ref, near_ref, far_ref, tiles_ref, qk_ref, out_ref):
    cross_attend(tile_rows, q_ref[...], near_ref, far_ref, tiles_ref, qk_ref, out_ref)


def cross_mix_from(tile_rows, queries, near, far, tiles, qk):
    return pl.pallas_call(
        functools.partial(attend_kernel, tile_rows),
        out_shape=jax.ShapeDtypeStruct(queries.shape, jnp.bfloat16),
        in_specs=[in_vmem()] * 5,
        out_specs=in_vmem(),
        compiler_params=params(),
    )(queries, near, far, tiles, qk)


def plain_query_kernel(section, gain_at, *refs):
    x_refs = refs[:GROUP]
    gain_ref, own_ref, other_ref, out_ref = refs[GROUP:]
    rows = out_ref.shape[0]
    project(section, gain_at, rows, x_refs, gain_ref, own_ref, other_ref, out_ref)


def plain_query_part(section, gain_at, rows, pieces, gains, own, other):
    return pl.pallas_call(
        functools.partial(plain_query_kernel, section, gain_at),
        out_shape=jax.ShapeDtypeStruct((rows, own.shape[1]), jnp.float32),
        in_specs=[in_vmem()] * (GROUP + 3),
        out_specs=in_vmem(),
        compiler_params=params(),
    )(*pieces, gains, own, other)


def turn(values, cosine, sine):
    half = HD // 2
    swapped = jnp.concatenate([values[:, half:], values[:, :half]], axis=1)
    return values * cosine + swapped * sine


def query_kernel(section, gain_at, *refs):
    x_refs = refs[:GROUP]
    gain_ref, cosine_ref, sine_ref, own_ref, other_ref, out_ref, product_ref = refs[GROUP:]
    rows = product_ref.shape[0]
    core = lax.axis_index("section")
    mine = pl.ds(pl.multiple_of(core * rows, rows), rows)
    queries = project(section, gain_at, rows, x_refs, gain_ref, own_ref, other_ref, product_ref)
    for head in range(queries.shape[1] // HD):
        turned = turn(queries[:, head * HD : (head + 1) * HD], cosine_ref[mine, :], sine_ref[mine, :])
        out_ref[head * rows : (head + 1) * rows, :] = turned.astype(jnp.bfloat16)


def query_part(section, gain_at, rows, pieces, gains, cosine, sine, own, other):
    columns = own.shape[1]
    return pl.pallas_call(
        functools.partial(query_kernel, section, gain_at),
        out_shape=jax.ShapeDtypeStruct((rows * columns // HD, HD), jnp.bfloat16),
        in_specs=[in_vmem()] * (GROUP + 5),
        out_specs=in_vmem(),
        scratch_shapes=[pltpu.VMEM((rows, columns), jnp.float32)],
        compiler_params=params(),
    )(*pieces, gains, cosine, sine, own, other)


def self_kernel(width, q_ref, near_ref, far_ref, cosine_ref, sine_ref, out_ref):
    core = lax.axis_index("section")
    rows = out_ref.shape[0]
    queries = q_ref[...]
    shape = (queries.shape[0], rows)
    row_at = lax.rem(lax.broadcasted_iota(jnp.int32, shape, 0), rows) + core * rows
    key_at = lax.broadcasted_iota(jnp.int32, shape, 1)
    keys, values, allowed, scales = [], [], [], []
    for ref, side in ((near_ref, core), (far_ref, 1 - core)):
        at = pl.ds(pl.multiple_of(side * rows, rows), rows)
        raw = ref[:rows, :HD].astype(jnp.float32)
        keys.append(turn(raw, cosine_ref[at, :], sine_ref[at, :]).astype(jnp.bfloat16))
        values.append(ref[:rows, HD:])
        allowed.append(key_at + side * rows <= row_at)
        square_sum = ref[rows : rows + 1, :rows].astype(jnp.float32)
        scales.append(lax.rsqrt(square_sum / width + epsilon))
    out_ref[...] = side_by_side(mix(queries, keys, values, allowed, scales), rows)


def self_mix(width, queries, near, far, cosine, sine):
    rows = cosine.shape[0] // 2
    return pl.pallas_call(
        functools.partial(self_kernel, width),
        out_shape=jax.ShapeDtypeStruct((rows, queries.shape[0] // rows * HD), jnp.bfloat16),
        in_specs=[in_vmem()] * 5,
        out_specs=in_vmem(),
        compiler_params=params(),
    )(queries, near, far, cosine, sine)


def key_value_kernel(section, hidden_ref, small_ref, own_ref, other_ref, out_ref, product):
    high = lax.axis_index("tp") // GROUP
    rows = hidden_ref.shape[0]
    hidden = hidden_ref[...].astype(jnp.float32)
    scaled = (hidden * small_ref[1:2, :]).astype(jnp.bfloat16)
    squares = hidden * hidden
    top = squares.astype(jnp.bfloat16)
    rest = (squares - top.astype(jnp.float32)).astype(jnp.bfloat16)
    ones = jnp.ones((16, hidden.shape[1]), jnp.bfloat16)
    square_sum = dot_rows(ones, top) + dot_rows(ones, rest)
    square_sum = jnp.concatenate(
        [square_sum, jnp.zeros((16, 2 * HD - rows), jnp.float32)], axis=1
    ).astype(jnp.bfloat16)

    def run(weight_ref):
        product[...] = jnp.dot(scaled, weight_ref[...], preferred_element_type=jnp.float32)

    with_weight(section, own_ref, other_ref, run)
    for k in range(GROUP):
        for part in range(2):
            start = pl.multiple_of((part * KV + (high ^ k)) * HD, HD)
            out_ref[k, :rows, part * HD : (part + 1) * HD] = product[:, pl.ds(start, HD)].astype(
                jnp.bfloat16
            )
        out_ref[k, rows:, :] = square_sum


def key_value_part(section, hidden, small, own, other):
    rows = hidden.shape[0]
    return pl.pallas_call(
        functools.partial(key_value_kernel, section),
        out_shape=jax.ShapeDtypeStruct((GROUP, rows + 16, 2 * HD), jnp.bfloat16),
        in_specs=[in_vmem()] * 4,
        out_specs=in_vmem(),
        scratch_shapes=[pltpu.VMEM((rows, own.shape[1]), jnp.float32)],
        compiler_params=params(),
    )(hidden, small, own, other)


def out_kernel(section, gated, *refs):
    x_refs = refs[:GROUP]
    hidden_ref, small_ref, tiles_ref, own_ref, other_ref, out_ref = refs[GROUP:]
    core = lax.axis_index("section")
    rows = out_ref.shape[0]
    depth = x_refs[0].shape[2]

    def run(weight_ref):
        branch = jnp.zeros(out_ref.shape, jnp.float32)
        for at in range(GROUP * GROUP):
            branch = branch + jnp.dot(
                x_refs[at // GROUP][at % GROUP],
                weight_rows(weight_ref, at, depth),
                preferred_element_type=jnp.float32,
            )
        if gated:
            row_tiles = tiles_ref[pl.ds(pl.multiple_of(core * rows, rows), rows), :1]
            branch = branch * (row_tiles > 0).astype(jnp.float32) * jnp.tanh(small_ref[3:4, :])
        out_ref[...] = (hidden_ref[...].astype(jnp.float32) + branch).astype(jnp.bfloat16)

    with_weight(section, own_ref, other_ref, run)


def out_part(section, gated, pieces, hidden, small, tiles, own, other):
    return pl.pallas_call(
        functools.partial(out_kernel, section, gated),
        out_shape=jax.ShapeDtypeStruct(hidden.shape, jnp.bfloat16),
        in_specs=[in_vmem()] * (GROUP + 5),
        out_specs=in_vmem(),
        compiler_params=params(),
    )(*pieces, hidden, small, tiles, own, other)


def encoder_kernel(states_ref, gain_ref, fc1_ref, fc2_ref, out_ref, product):
    core = lax.axis_index("section")
    chip = lax.axis_index("tp")
    member = jnp.where(core == 0, chip % GROUP, chip // GROUP)
    states = states_ref[...].astype(jnp.float32)
    centred = states - jnp.mean(states, axis=-1, keepdims=True)
    spread = jnp.mean(centred * centred, axis=-1, keepdims=True)
    normed = (centred * lax.rsqrt(spread + epsilon) * gain_ref[...]).astype(jnp.bfloat16)
    inner = jnp.dot(normed, fc1_ref[...], preferred_element_type=jnp.float32)
    inner = (0.5 * inner * (1.0 + lax.erf(inner * 2.0 ** (-0.5)))).astype(jnp.bfloat16)
    product[...] = jnp.dot(inner, fc2_ref[...], preferred_element_type=jnp.float32).astype(
        jnp.bfloat16
    )
    rows = out_ref.shape[1]
    for k in range(GROUP):
        out_ref[k] = product[pl.ds(pl.multiple_of((member ^ k) * rows, rows), rows), :]


def encoder_part(states, gain, fc1, fc2):
    rows, width = states.shape
    return pl.pallas_call(
        encoder_kernel,
        out_shape=jax.ShapeDtypeStruct((GROUP, rows // GROUP, width), jnp.bfloat16),
        in_specs=[in_vmem()] * 4,
        out_specs=in_vmem(),
        scratch_shapes=[pltpu.VMEM((rows, width), jnp.bfloat16)],
        compiler_params=params(),
    )(states, gain, fc1, fc2)


def image_kernel(p0, p1, p2, p3, projector_ref, own_ref, other_ref, out_ref, rows_ref, kv_ref):
    core = lax.axis_index("section")
    chip = lax.axis_index("tp")
    low, high = chip % GROUP, chip // GROUP
    member = jnp.where(core == 0, low, high)
    count = p0.shape[0]
    for k, ref in enumerate((p0, p1, p2, p3)):
        rows_ref[pl.ds(pl.multiple_of((member ^ k) * count, count), count), :] = ref[...]
    feats = jnp.dot(
        rows_ref[...], projector_ref[...], preferred_element_type=jnp.float32
    ).astype(jnp.bfloat16)
    for section in range(2):
        weight = jnp.where(core == section, own_ref[...], other_ref[...])
        kv_ref[...] = jnp.dot(feats, weight, preferred_element_type=jnp.float32)
        for k in range(GROUP):
            head = high ^ k
            for part in range(2):
                start = pl.multiple_of((part * KV + head) * HD, HD)
                out_ref[section, k, :, part * HD : (part + 1) * HD] = kv_ref[
                    :, pl.ds(start, HD)
                ].astype(jnp.bfloat16)


def image_part(pieces, projector, own, other):
    rows = GROUP * pieces[0].shape[0]
    return pl.pallas_call(
        image_kernel,
        out_shape=jax.ShapeDtypeStruct((2, GROUP, rows, 2 * HD), jnp.bfloat16),
        in_specs=[in_vmem()] * 7,
        out_specs=in_vmem(),
        scratch_shapes=[
            pltpu.VMEM((rows, projector.shape[0]), jnp.bfloat16),
            pltpu.VMEM((rows, own.shape[1]), jnp.float32),
        ],
        compiler_params=params(),
    )(*pieces, projector, own, other)


def rope_tables(positions):
    inverse = 500000.0 ** (-np.arange(HD // 2) * (2.0 / HD))
    angles = np.arange(positions)[:, None] * inverse[None, :]
    cosine, sine = np.cos(angles), np.sin(angles)
    return (
        np.concatenate([cosine, cosine], axis=1).astype(np.float32),
        np.concatenate([-sine, sine], axis=1).astype(np.float32),
    )


def paired_body(
    text_states,
    vision_states,
    visible_tiles,
    vision_norm_gain,
    vision_fc1,
    vision_fc2,
    vision_gate,
    projector,
    cross_norm,
    cross_q,
    cross_kv,
    cross_qk_gain,
    cross_o,
    cross_gate,
    self_norm,
    self_q,
    self_kv,
    self_o,
):
    core = lax.axis_index("section")
    chip = lax.axis_index("tp")
    seq_len, local_width = text_states.shape
    rows = seq_len // 2
    full_width = local_width * lax.axis_size("tp")
    member = jnp.where(core == 0, chip % GROUP, chip // GROUP)

    small = jnp.concatenate(
        [
            cross_norm.astype(jnp.float32),
            self_norm.astype(jnp.float32),
            jnp.pad(cross_qk_gain.reshape(1, -1), ((0, 0), (0, local_width - 2 * HD))),
            jnp.broadcast_to(cross_gate[None], (1, local_width)),
        ]
    )
    small = lax.all_gather(small, "section", axis=0)
    own_cross_kv, own_cross_q, own_cross_o = cross_kv[0], cross_q[0], cross_o[0]
    own_self_kv, own_self_q, own_self_o = self_kv[0], self_q[0], self_o[0]
    far_cross_kv = swap_cores(own_cross_kv)
    far_cross_q = swap_cores(own_cross_q)
    far_cross_o = swap_cores(own_cross_o)
    far_self_kv = swap_cores(own_self_kv)
    far_self_q = swap_cores(own_self_q)
    far_self_o = swap_cores(own_self_o)

    hidden = lax.dynamic_slice_in_dim(text_states, core * rows, rows, 0)
    gain_rows = small[:, :2].astype(jnp.bfloat16).reshape(4, local_width)
    entry = jnp.concatenate(
        [hidden, gain_rows, jnp.zeros((12, local_width), jnp.bfloat16)], axis=0
    )
    come = [send_xor(entry, (GROUP * k, k)) for k in range(1, GROUP)]

    branch = encoder_part(vision_states, vision_norm_gain[None], vision_fc1, vision_fc2)
    branch, come = lax.optimization_barrier((branch, come))
    first = jnp.stack([entry] + come)
    pieces = [first] + [send_xor(first, (k, GROUP * k)) for k in range(1, GROUP)]
    near = total(
        [branch[0]] + [send_xor(branch[k], (k, GROUP * k)) for k in range(1, GROUP)]
    ).astype(jnp.bfloat16)
    come = [send_xor(near, (GROUP * k, k)) for k in range(1, GROUP)]
    come, pieces = lax.optimization_barrier((come, pieces))
    gains = jnp.concatenate([piece[:, rows:] for piece in pieces], axis=0)
    branch_rows = total([near] + come)
    vis_rows = lax.dynamic_index_in_dim(
        vision_states.reshape(branch.shape), member, 0, keepdims=False
    )
    vis_out = (vis_rows.astype(jnp.float32) + jnp.tanh(vision_gate[0]) * branch_rows).astype(
        jnp.bfloat16
    )
    come = [send_xor(vis_out, (k, GROUP * k)) for k in range(1, GROUP)]
    queries = plain_query_part(0, 0, rows, pieces, gains, own_cross_q, far_cross_q)
    come, queries = lax.optimization_barrier((come, queries))
    vis_pieces = [vis_out] + come

    image_parts = image_part(vis_pieces, projector, own_cross_kv, far_cross_kv)
    image_kv = []
    for section in range(2):
        kv_rows = reduce_heads(image_parts[section])
        key_gain = small[section, 2, HD : 2 * HD]
        near = jnp.concatenate(
            [rms_norm(kv_rows[:, :HD], key_gain), kv_rows[:, HD:]], axis=1
        ).astype(jnp.bfloat16)
        image_kv.append((near, swap_cores(near)))

    tile_rows = 2 * vision_states.shape[0] // TILES
    tiles = jnp.broadcast_to(visible_tiles[:, None], (seq_len, HD))
    cosine, sine = (jnp.asarray(table) for table in rope_tables(seq_len))

    results = []
    for section in range(2):
        scalars = small[section]
        near, far = image_kv[section]
        if section == 0:
            mixed = cross_mix_from(tile_rows, queries, near, far, tiles, scalars)
        else:
            mixed = cross_mix(
                section, 2 * section, tile_rows, rows, gather_chips(hidden), gains, near, far,
                tiles, scalars, own_cross_q, far_cross_q,
            )
        hidden = out_part(
            section, True, gather_chips(mixed), hidden, scalars, tiles, own_cross_o, far_cross_o
        )
        pieces = gather_chips(hidden)
        near = reduce_heads(
            key_value_part(section, hidden, scalars, own_self_kv, far_self_kv)
        ).astype(jnp.bfloat16)
        far = swap_cores(near)
        queries = query_part(
            section, 2 * section + 1, rows, pieces, gains, cosine, sine, own_self_q, far_self_q
        )
        mixed = self_mix(full_width, queries, near, far, cosine, sine)
        hidden = out_part(
            section, False, gather_chips(mixed), hidden, scalars, tiles, own_self_o, far_self_o
        )
        results.append(hidden)
    come = swap_cores(jnp.where(core == 0, results[1], results[0]))
    return jnp.where(
        core == 0,
        jnp.concatenate([results[0], come], axis=0),
        jnp.concatenate([come, results[1]], axis=0),
    )[None]


def solution(mesh):
    chips = mesh.shape["tp"]
    paired = mesh.shape["section"] == 2 and chips == GROUP * GROUP and HEADS == 2 * chips
    body = paired_body if paired else blocked_body
    in_specs = (
        P(None, "tp"),
        P("section", None),
        P(),
        P(),
        P(None, "tp"),
        P("tp", None),
        P(),
        P(None, "tp"),
        P("section", "tp"),
        P("section", None, "tp"),
        P("section", "tp", None),
        P("section", None, None),
        P("section", None, "tp"),
        P("section"),
        P("section", "tp"),
        P("section", None, "tp"),
        P("section", "tp", None),
        P("section", None, "tp"),
    )
    out_specs = P("section", None, "tp")
    return jax.shard_map(body, mesh=mesh, in_specs=in_specs, out_specs=out_specs, check_vma=False)
```

```python
import functools

import jax
import jax.numpy as jnp
import numpy as np
from jax import lax
from jax.experimental import pallas as pl
from jax.experimental.pallas import tpu as pltpu
from jax.sharding import PartitionSpec as P

HD = 128
HEADS = 32
KV = 4
TILES = 4
ROWS = 64
BLOCKS = 2


epsilon = 1e-05


def from_behind(block, axis, distance):
    devices = range(lax.axis_size(axis))
    route = [(i - distance, i) for i in devices if i - distance in devices]
    return lax.ppermute(block, axis, route)


def rms_norm(values, gain_row):
    mean_square = jnp.mean(values * values, axis=-1, keepdims=True)
    return values * lax.rsqrt(mean_square + epsilon) * gain_row.astype(jnp.float32)


def rotate(values, positions):
    half_dim = values.shape[-1] // 2
    exponents = jnp.arange(half_dim, dtype=jnp.float32) * (2.0 / values.shape[-1])
    inverse = jnp.float32(500000.0) ** (-exponents)
    angles = positions.astype(jnp.float32)[:, None] * inverse[None, :]
    cosine = jnp.cos(angles)[:, None, :]
    sine = jnp.sin(angles)[:, None, :]
    lower = values[..., :half_dim]
    upper = values[..., half_dim:]
    return jnp.concatenate([lower * cosine - upper * sine, upper * cosine + lower * sine], axis=-1)


def softmax_rows(scores):
    top_score = jnp.max(scores, axis=-1, keepdims=True)
    raised = jnp.exp(scores - top_score)
    return raised / jnp.sum(raised, axis=-1, keepdims=True)


def head_columns(kv_rows, kv_head):
    key_part = lax.dynamic_slice_in_dim(kv_rows, kv_head * HD, HD, 1)
    value_part = lax.dynamic_slice_in_dim(kv_rows, (KV + kv_head) * HD, HD, 1)
    return (key_part, value_part)


def attend_one(queries, key_rows, value_rows, allowed):
    scores = jnp.einsum(
        "rhd,jd->hrj", queries, key_rows, preferred_element_type=jnp.float32
    ) * HD ** (-0.5)
    scores = jnp.where(allowed[None], scores, -1e30)
    weights = softmax_rows(scores).astype(jnp.bfloat16)
    mixed_heads = jnp.einsum("hrj,jd->rhd", weights, value_rows, preferred_element_type=jnp.float32)
    return mixed_heads.astype(jnp.bfloat16).reshape(queries.shape[0], -1)


def out_fold(weight, segment):
    return jnp.dot(segment, weight, preferred_element_type=jnp.float32)


def blocked_body(
    text_states,
    vision_states,
    visible_tiles,
    vision_norm_gain,
    vision_fc1,
    vision_fc2,
    vision_gate,
    projector,
    cross_norm,
    cross_q,
    cross_kv,
    cross_qk_gain,
    cross_o,
    cross_gate,
    self_norm,
    self_q,
    self_kv,
    self_o,
):
    section_idx = lax.axis_index("section")
    section_total = lax.axis_size("section")
    tp_index = lax.axis_index("tp")
    local_width = text_states.shape[1]
    heads_local = cross_q.shape[2] // HD
    kv_group = HEADS // KV
    kv_head = tp_index * heads_local // kv_group
    vis_f32 = vision_states.astype(jnp.float32)
    centre = jnp.mean(vis_f32, axis=-1, keepdims=True)
    spread = jnp.mean((vis_f32 - centre) ** 2, axis=-1, keepdims=True)
    normed_vis = ((vis_f32 - centre) * lax.rsqrt(spread + epsilon) * vision_norm_gain).astype(
        jnp.bfloat16
    )
    vis_hidden = jax.nn.gelu(
        jnp.dot(normed_vis, vision_fc1, preferred_element_type=jnp.float32), approximate=False
    ).astype(jnp.bfloat16)
    vis_branch = lax.psum(jnp.dot(vis_hidden, vision_fc2, preferred_element_type=jnp.float32), "tp")
    vis_out = (vis_f32 + jnp.tanh(vision_gate[0]) * vis_branch).astype(jnp.bfloat16)
    every_row = lax.all_gather(vis_out, "section", axis=0, tiled=True)
    image_feats = jnp.dot(every_row, projector, preferred_element_type=jnp.float32).astype(
        jnp.bfloat16
    )
    image_count = image_feats.shape[0]
    kv_term = jnp.dot(image_feats, cross_kv[0], preferred_element_type=jnp.float32)
    key_gain = cross_qk_gain[0, 1]
    kv_image = lax.psum(kv_term, "tp")
    key_part, value_part = head_columns(kv_image, kv_head)
    key_img = rms_norm(key_part, key_gain).astype(jnp.bfloat16)
    val_img = value_part.astype(jnp.bfloat16)
    tile_of = jnp.arange(image_count, dtype=jnp.int32) // (image_count // TILES)
    seq_len = text_states.shape[0]
    positions_all = jnp.arange(seq_len, dtype=jnp.int32)
    gate_cross = jnp.tanh(cross_gate[0])
    key_cache = jnp.zeros((seq_len, HD), jnp.bfloat16)
    val_cache = jnp.zeros((seq_len, HD), jnp.bfloat16)
    outputs = jnp.zeros((seq_len, local_width), jnp.bfloat16)
    incoming = jnp.zeros((ROWS, local_width), jnp.bfloat16)
    step_count = BLOCKS + section_total - 1
    for step_no in range(step_count):
        block_idx = step_no - section_idx
        is_live = (block_idx >= 0) & (block_idx < BLOCKS)
        row_start = jnp.clip(block_idx, 0, BLOCKS - 1) * ROWS
        entry_block = min(step_no, BLOCKS - 1)
        first_rows = text_states[entry_block * ROWS : (entry_block + 1) * ROWS]
        current = jnp.where(section_idx == 0, first_rows, incoming)
        positions = row_start + jnp.arange(ROWS, dtype=jnp.int32)
        whole_rows, gain_row = (
            lax.all_gather(current, "tp", axis=1, tiled=True),
            lax.all_gather(cross_norm, "tp", axis=1, tiled=True),
        )
        normed = rms_norm(whole_rows.astype(jnp.float32), gain_row[0]).astype(jnp.bfloat16)
        queries = jnp.dot(normed, cross_q[0], preferred_element_type=jnp.float32).reshape(
            ROWS, heads_local, HD
        )
        queries = rms_norm(queries, cross_qk_gain[0, 0]).astype(jnp.bfloat16)
        row_tiles = lax.dynamic_slice_in_dim(visible_tiles, row_start, ROWS)
        allowed = tile_of[None, :] < row_tiles[:, None]
        mixed_heads = attend_one(queries, key_img, val_img, allowed)
        cross_branch = out_fold(cross_o[0], lax.all_gather(mixed_heads, "tp", axis=1, tiled=True))
        cross_branch = cross_branch * (row_tiles > 0).astype(jnp.float32)[:, None]
        current = (current.astype(jnp.float32) + gate_cross * cross_branch).astype(jnp.bfloat16)
        whole_rows, gain_row = (
            lax.all_gather(current, "tp", axis=1, tiled=True),
            lax.all_gather(self_norm, "tp", axis=1, tiled=True),
        )
        normed = rms_norm(whole_rows.astype(jnp.float32), gain_row[0]).astype(jnp.bfloat16)
        queries = rotate(
            jnp.dot(normed, self_q[0], preferred_element_type=jnp.float32).reshape(
                ROWS, heads_local, HD
            ),
            positions,
        ).astype(jnp.bfloat16)
        own_cols = lax.dynamic_slice_in_dim(normed, tp_index * local_width, local_width, 1)
        kv_text = lax.psum(
            jnp.dot(own_cols, self_kv[0], preferred_element_type=jnp.float32).astype(jnp.bfloat16),
            "tp",
        ).astype(jnp.float32)
        key_part, value_part = head_columns(kv_text, kv_head)
        new_keys = rotate(key_part[:, None, :], positions)[:, 0].astype(jnp.bfloat16)
        new_vals = value_part.astype(jnp.bfloat16)
        key_cache = jnp.where(
            is_live, lax.dynamic_update_slice_in_dim(key_cache, new_keys, row_start, 0), key_cache
        )
        val_cache = jnp.where(
            is_live, lax.dynamic_update_slice_in_dim(val_cache, new_vals, row_start, 0), val_cache
        )
        causal = positions_all[None, :] <= positions[:, None]
        mixed_heads = attend_one(queries, key_cache, val_cache, causal)
        self_branch = out_fold(self_o[0], lax.all_gather(mixed_heads, "tp", axis=1, tiled=True))
        current = (current.astype(jnp.float32) + self_branch).astype(jnp.bfloat16)
        outputs = jnp.where(
            is_live, lax.dynamic_update_slice_in_dim(outputs, current, row_start, 0), outputs
        )
        if step_no + 1 < step_count:
            incoming = from_behind(current, "section", 1)
    return outputs[None]


VMEM_LIMIT = 11 * 1024 * 1024
GROUP = 4


def params(limit=VMEM_LIMIT):
    return pltpu.CompilerParams(vmem_limit_bytes=limit)


def in_vmem():
    return pl.BlockSpec(memory_space=pltpu.VMEM)


def swap_cores(block):
    return lax.ppermute(block, "section", [(0, 1), (1, 0)])


def send_xor(block, masks):
    chips = lax.axis_size("tp")
    route = [
        (core * chips + chip, core * chips + (chip ^ masks[core]))
        for core in range(2)
        for chip in range(chips)
    ]
    return lax.ppermute(block, ("section", "tp"), route)


def send_group(blocks, scale):
    order = range(GROUP - 1, 0, -1)
    sent = {k: send_xor(blocks[k], (scale[0] * k, scale[1] * k)) for k in order}
    return [sent[k] for k in range(1, GROUP)]


def gather_chips(block, beside_first=None, beside_second=None):
    after = lax.optimization_barrier
    come = send_group([block] * GROUP, (GROUP, 1))
    extras = []
    if beside_first is not None:
        come, extra = after((come, beside_first()))
        extras.append(extra)
    first = jnp.stack([block] + come)
    come = send_group([first] * GROUP, (1, GROUP))
    if beside_second is not None:
        come, extra = after((come, beside_second(extras[0])))
        extras.append(extra)
    return [first] + come, extras


def total(parts):
    return sum((part.astype(jnp.float32) for part in parts[1:]), parts[0].astype(jnp.float32))


def head_steps(blocks):
    def fold(kept, come):
        return (kept.astype(jnp.float32) + come.astype(jnp.float32)).astype(jnp.bfloat16)

    return [
        lambda: send_xor(blocks[2:], (2 * GROUP, 2 * GROUP)),
        lambda come: fold(blocks[:2], come),
        lambda rows: send_xor(rows[1], (GROUP, GROUP)),
        lambda rows, come: fold(rows[0], come),
        lambda rows: send_xor(rows, (1, 1)),
        lambda rows, come: fold(rows, come),
        lambda rows: send_xor(rows, (2, 2)),
        lambda rows, come: rows.astype(jnp.float32) + come.astype(jnp.float32),
    ]


def gather_mask(core, at):
    outer, inner = divmod(at, GROUP)
    return outer ^ GROUP * inner if core == 0 else inner ^ GROUP * outer


def text_mask(core, at):
    outer, inner = divmod(at, GROUP)
    return (outer if core == 0 else outer % 2 * 2 + outer // 2) ^ GROUP * inner


def with_weight(section, own, other, run):
    core = lax.axis_index("section")

    @pl.when(core == section)
    def _():
        run(section, *own)

    @pl.when(core != section)
    def _():
        run(1 - section, *other)


def weight_rows(weight_ref, mask, rows):
    source = lax.axis_index("tp") ^ mask
    return weight_ref[pl.ds(pl.multiple_of(source * rows, rows), rows), :]


def project(section, gain_at, rows, x_refs, gain_refs, weight_refs, product_ref, mask_of=gather_mask):
    depth = x_refs[0].shape[2]
    pieces = range(GROUP * GROUP)
    gain_place = {text_mask(section, at): at for at in pieces}

    def run(core, gain_ref, weight_ref):
        product = jnp.zeros(product_ref.shape, jnp.float32)
        squares = jnp.zeros((rows, depth), jnp.float32)
        for at in pieces:
            mask = mask_of(core, at)
            piece = x_refs[at // GROUP][at % GROUP, :rows, :].astype(jnp.float32)
            squares = squares + piece * piece
            gain_row = gain_ref[gain_place[mask], gain_at : gain_at + 1, :].astype(jnp.float32)
            scaled = (piece * gain_row).astype(jnp.bfloat16)
            product = product + jnp.dot(
                scaled, weight_rows(weight_ref, mask, depth), preferred_element_type=jnp.float32
            )
        mean_square = jnp.sum(squares, axis=1, keepdims=True) / (GROUP * GROUP * depth)
        product_ref[...] = product * lax.rsqrt(mean_square + epsilon)

    with_weight(
        section, (gain_refs[0], weight_refs[0]), (gain_refs[1], weight_refs[1]), run
    )
    return product_ref[...]


def dot_rows(left, right):
    return lax.dot_general(
        left, right, (((1,), (1,)), ((), ())), preferred_element_type=jnp.float32
    )


def mix(queries, key_sets, value_sets, allowed_sets, value_scales):
    scores = []
    for keys, allowed, scale in zip(key_sets, allowed_sets, value_scales):
        part = dot_rows(queries, keys) * HD ** (-0.5)
        if scale is not None:
            part = part * scale
        scores.append(jnp.where(allowed, part, -1e30))
    top = functools.reduce(
        jnp.maximum, [jnp.max(part, axis=1, keepdims=True) for part in scores]
    )
    raised = [jnp.exp(part - top) for part in scores]
    bottom = sum(jnp.sum(part, axis=1, keepdims=True) for part in raised)
    mixed = jnp.zeros(queries.shape, jnp.float32)
    for part, values, scale in zip(raised, value_sets, value_scales):
        weights = part / bottom
        if scale is not None:
            weights = weights * scale
        mixed = mixed + jnp.dot(
            weights.astype(jnp.bfloat16), values, preferred_element_type=jnp.float32
        )
    return mixed.astype(jnp.bfloat16)


def by_head(queries):
    heads = queries.shape[1] // HD
    return jnp.concatenate([queries[:, h * HD : (h + 1) * HD] for h in range(heads)], axis=0)


def side_by_side(mixed, rows):
    return jnp.concatenate(
        [mixed[start : start + rows] for start in range(0, mixed.shape[0], rows)], axis=1
    )


def cross_attend(tile_rows, queries, near_ref, far_ref, tiles_ref, qk_ref, out_ref):
    core = lax.axis_index("section")
    rows = out_ref.shape[0]
    queries = rms_norm(by_head(queries), qk_ref[1:2, :HD]).astype(jnp.bfloat16)
    row_tiles = tiles_ref[pl.ds(pl.multiple_of(core * rows, rows), rows), :]
    row_tiles = jnp.concatenate([row_tiles] * (queries.shape[0] // rows), axis=0)
    count = near_ref.shape[0]
    key_at = lax.broadcasted_iota(jnp.int32, (queries.shape[0], count), 1)
    allowed = [
        key_at + core * count < row_tiles * tile_rows,
        key_at + (1 - core) * count < row_tiles * tile_rows,
    ]
    sets = (near_ref[...], far_ref[...])
    mixed = mix(
        queries, [kv[:, :HD] for kv in sets], [kv[:, HD:] for kv in sets], allowed, (None, None)
    )
    out_ref[...] = side_by_side(mixed, rows)


def cross_kernel(section, gain_at, tile_rows, *refs):
    x_refs = refs[:GROUP]
    gain_refs, weight_refs = refs[GROUP : GROUP + 2], refs[GROUP + 2 : GROUP + 4]
    near_ref, far_ref, tiles_ref, qk_ref, out_ref, product_ref = refs[GROUP + 4 :]
    rows = out_ref.shape[0]
    queries = project(section, gain_at, rows, x_refs, gain_refs, weight_refs, product_ref)
    cross_attend(tile_rows, queries, near_ref, far_ref, tiles_ref, qk_ref, out_ref)


def cross_mix(section, gain_at, tile_rows, rows, pieces, gains, weights, near, far, tiles, qk):
    columns = weights[0].shape[1]
    return pl.pallas_call(
        functools.partial(cross_kernel, section, gain_at, tile_rows),
        out_shape=jax.ShapeDtypeStruct((rows, columns), jnp.bfloat16),
        in_specs=[in_vmem()] * (GROUP + 8),
        out_specs=in_vmem(),
        scratch_shapes=[pltpu.VMEM((rows, columns), jnp.float32)],
        compiler_params=params(),
    )(*pieces, *gains, *weights, near, far, tiles, qk)


def attend_kernel(tile_rows, q_ref, near_ref, far_ref, tiles_ref, qk_ref, out_ref):
    cross_attend(tile_rows, q_ref[...], near_ref, far_ref, tiles_ref, qk_ref, out_ref)


def cross_mix_from(tile_rows, queries, near, far, tiles, qk):
    return pl.pallas_call(
        functools.partial(attend_kernel, tile_rows),
        out_shape=jax.ShapeDtypeStruct(queries.shape, jnp.bfloat16),
        in_specs=[in_vmem()] * 5,
        out_specs=in_vmem(),
        compiler_params=params(),
    )(queries, near, far, tiles, qk)


def plain_query_kernel(section, gain_at, *refs):
    x_refs, gain_refs, weight_refs, out_ref = refs[:-5], refs[-5:-3], refs[-3:-1], refs[-1]
    rows = out_ref.shape[0]
    project(section, gain_at, rows, x_refs, gain_refs, weight_refs, out_ref, text_mask)


def plain_query_part(section, gain_at, rows, pieces, gains, weights):
    return pl.pallas_call(
        functools.partial(plain_query_kernel, section, gain_at),
        out_shape=jax.ShapeDtypeStruct((rows, weights[0].shape[1]), jnp.float32),
        in_specs=[in_vmem()] * (len(pieces) + 4),
        out_specs=in_vmem(),
        compiler_params=params(),
    )(*pieces, *gains, *weights)


def turn(values, cosine, sine):
    half = HD // 2
    swapped = jnp.concatenate([values[:, half:], values[:, :half]], axis=1)
    return values * cosine + swapped * sine


def query_kernel(section, gain_at, *refs):
    x_refs, gain_refs, weight_refs = refs[:GROUP], refs[GROUP : GROUP + 2], refs[GROUP + 2 : GROUP + 4]
    cosine_ref, sine_ref, out_ref, product_ref = refs[GROUP + 4 :]
    rows = product_ref.shape[0]
    core = lax.axis_index("section")
    mine = pl.ds(pl.multiple_of(core * rows, rows), rows)
    queries = project(section, gain_at, rows, x_refs, gain_refs, weight_refs, product_ref)
    for head in range(queries.shape[1] // HD):
        turned = turn(queries[:, head * HD : (head + 1) * HD], cosine_ref[mine, :], sine_ref[mine, :])
        out_ref[head * rows : (head + 1) * rows, :] = turned.astype(jnp.bfloat16)


def query_part(section, gain_at, rows, pieces, gains, weights, cosine, sine):
    columns = weights[0].shape[1]
    return pl.pallas_call(
        functools.partial(query_kernel, section, gain_at),
        out_shape=jax.ShapeDtypeStruct((rows * columns // HD, HD), jnp.bfloat16),
        in_specs=[in_vmem()] * (GROUP + 6),
        out_specs=in_vmem(),
        scratch_shapes=[pltpu.VMEM((rows, columns), jnp.float32)],
        compiler_params=params(),
    )(*pieces, *gains, *weights, cosine, sine)


def self_kernel(width, q_ref, near_ref, far_ref, cosine_ref, sine_ref, out_ref):
    core = lax.axis_index("section")
    rows = out_ref.shape[0]
    queries = q_ref[...]
    shape = (queries.shape[0], rows)
    row_at = lax.rem(lax.broadcasted_iota(jnp.int32, shape, 0), rows) + core * rows
    key_at = lax.broadcasted_iota(jnp.int32, shape, 1)
    keys, values, allowed, scales = [], [], [], []
    for ref, side in ((near_ref, core), (far_ref, 1 - core)):
        at = pl.ds(pl.multiple_of(side * rows, rows), rows)
        raw = ref[:rows, :HD].astype(jnp.float32)
        keys.append(turn(raw, cosine_ref[at, :], sine_ref[at, :]).astype(jnp.bfloat16))
        values.append(ref[:rows, HD:])
        allowed.append(key_at + side * rows <= row_at)
        square_sum = ref[rows : rows + 1, :rows].astype(jnp.float32)
        scales.append(lax.rsqrt(square_sum / width + epsilon))
    out_ref[...] = side_by_side(mix(queries, keys, values, allowed, scales), rows)


def self_mix(width, queries, near, far, cosine, sine):
    rows = cosine.shape[0] // 2
    return pl.pallas_call(
        functools.partial(self_kernel, width),
        out_shape=jax.ShapeDtypeStruct((rows, queries.shape[0] // rows * HD), jnp.bfloat16),
        in_specs=[in_vmem()] * 5,
        out_specs=in_vmem(),
        compiler_params=params(),
    )(queries, near, far, cosine, sine)


def key_value_kernel(section, hidden_ref, small_ref, own_ref, other_ref, out_ref, product):
    high = lax.axis_index("tp") // GROUP
    rows = hidden_ref.shape[0]
    hidden = hidden_ref[...].astype(jnp.float32)
    scaled = (hidden * small_ref[0:1, :]).astype(jnp.bfloat16)
    squares = hidden * hidden
    top = squares.astype(jnp.bfloat16)
    rest = (squares - top.astype(jnp.float32)).astype(jnp.bfloat16)
    ones = jnp.ones((16, hidden.shape[1]), jnp.bfloat16)
    square_sum = dot_rows(ones, top) + dot_rows(ones, rest)
    square_sum = jnp.concatenate(
        [square_sum, jnp.zeros((16, 2 * HD - rows), jnp.float32)], axis=1
    ).astype(jnp.bfloat16)

    def run(core, weight_ref):
        product[...] = jnp.dot(scaled, weight_ref[...], preferred_element_type=jnp.float32)

    with_weight(section, (own_ref,), (other_ref,), run)
    for k in range(GROUP):
        for part in range(2):
            start = pl.multiple_of((part * KV + (high ^ k)) * HD, HD)
            out_ref[k, :rows, part * HD : (part + 1) * HD] = product[:, pl.ds(start, HD)].astype(
                jnp.bfloat16
            )
        out_ref[k, rows:, :] = square_sum


def key_value_part(section, hidden, small, own, other):
    rows = hidden.shape[0]
    return pl.pallas_call(
        functools.partial(key_value_kernel, section),
        out_shape=jax.ShapeDtypeStruct((GROUP, rows + 16, 2 * HD), jnp.bfloat16),
        in_specs=[in_vmem()] * 4,
        out_specs=in_vmem(),
        scratch_shapes=[pltpu.VMEM((rows, own.shape[1]), jnp.float32)],
        compiler_params=params(),
    )(hidden, small, own, other)


def out_kernel(section, gated, *refs):
    x_refs = refs[:GROUP]
    hidden_ref, small_ref, tiles_ref, own_ref, other_ref, out_ref = refs[GROUP:]
    rows = out_ref.shape[0]
    depth = x_refs[0].shape[2]

    def run(core, weight_ref):
        branch = jnp.zeros(out_ref.shape, jnp.float32)
        for at in range(GROUP * GROUP):
            branch = branch + jnp.dot(
                x_refs[at // GROUP][at % GROUP],
                weight_rows(weight_ref, gather_mask(core, at), depth),
                preferred_element_type=jnp.float32,
            )
        if gated:
            row_tiles = tiles_ref[core * rows : (core + 1) * rows, :1]
            branch = branch * (row_tiles > 0).astype(jnp.float32) * jnp.tanh(small_ref[2:3, :])
        out_ref[...] = (hidden_ref[...].astype(jnp.float32) + branch).astype(jnp.bfloat16)

    with_weight(section, (own_ref,), (other_ref,), run)


def out_part(section, gated, pieces, hidden, small, tiles, own, other):
    return pl.pallas_call(
        functools.partial(out_kernel, section, gated),
        out_shape=jax.ShapeDtypeStruct(hidden.shape, jnp.bfloat16),
        in_specs=[in_vmem()] * (GROUP + 5),
        out_specs=in_vmem(),
        compiler_params=params(),
    )(*pieces, hidden, small, tiles, own, other)


def encoder_kernel(states_hbm, gain_ref, fc1_hbm, fc2_hbm, out_ref, states_ref, fc1_ref, fc2_ref, product, sems):
    copies = [
        pltpu.make_async_copy(source, target, sems.at[at])
        for at, (source, target) in enumerate(
            ((states_hbm, states_ref), (fc1_hbm, fc1_ref), (fc2_hbm, fc2_ref))
        )
    ]
    for copy in copies:
        copy.start()
    core = lax.axis_index("section")
    chip = lax.axis_index("tp")
    member = jnp.where(core == 0, chip % GROUP, chip // GROUP)
    copies[0].wait()
    states = states_ref[...].astype(jnp.float32)
    centred = states - jnp.mean(states, axis=-1, keepdims=True)
    spread = jnp.mean(centred * centred, axis=-1, keepdims=True)
    normed = (centred * lax.rsqrt(spread + epsilon) * gain_ref[...]).astype(jnp.bfloat16)
    copies[1].wait()
    inner = dot_rows(normed, fc1_ref[...])
    inner = (0.5 * inner * (1.0 + lax.erf(inner * 2.0 ** (-0.5)))).astype(jnp.bfloat16)
    copies[2].wait()
    product[...] = jnp.dot(inner, fc2_ref[...], preferred_element_type=jnp.float32).astype(
        jnp.bfloat16
    )
    rows = out_ref.shape[1]
    for k in range(GROUP):
        out_ref[k] = product[pl.ds(pl.multiple_of((member ^ k) * rows, rows), rows), :]


def encoder_part(states, gain, fc1, fc2):
    rows, width = states.shape
    in_place = pl.BlockSpec(memory_space=pltpu.HBM)
    return pl.pallas_call(
        encoder_kernel,
        out_shape=jax.ShapeDtypeStruct((GROUP, rows // GROUP, width), jnp.bfloat16),
        in_specs=[in_place, in_vmem(), in_place, in_place],
        out_specs=in_vmem(),
        scratch_shapes=[
            pltpu.VMEM(states.shape, jnp.bfloat16),
            pltpu.VMEM(fc1.shape, jnp.bfloat16),
            pltpu.VMEM(fc2.shape, jnp.bfloat16),
            pltpu.VMEM((rows, width), jnp.bfloat16),
            pltpu.SemaphoreType.DMA((3,)),
        ],
        compiler_params=params(5 * VMEM_LIMIT),
    )(states, gain, fc1, fc2)


def image_kernel(p0, p1, p2, p3, projector_ref, own_ref, other_ref, out_ref, rows_ref, kv_ref):
    core = lax.axis_index("section")
    chip = lax.axis_index("tp")
    low, high = chip % GROUP, chip // GROUP
    member = jnp.where(core == 0, low, high)
    count = p0.shape[0]
    for k, ref in enumerate((p0, p1, p2, p3)):
        rows_ref[pl.ds(pl.multiple_of((member ^ k) * count, count), count), :] = ref[...]
    feats = jnp.dot(
        rows_ref[...], projector_ref[...], preferred_element_type=jnp.float32
    ).astype(jnp.bfloat16)
    for section in range(2):
        weight = jnp.where(core == section, own_ref[...], other_ref[...])
        kv_ref[...] = jnp.dot(feats, weight, preferred_element_type=jnp.float32)
        for k in range(GROUP):
            head = high ^ k
            for part in range(2):
                start = pl.multiple_of((part * KV + head) * HD, HD)
                out_ref[section, k, :, part * HD : (part + 1) * HD] = kv_ref[
                    :, pl.ds(start, HD)
                ].astype(jnp.bfloat16)


def image_part(pieces, projector, own, other):
    rows = GROUP * pieces[0].shape[0]
    return pl.pallas_call(
        image_kernel,
        out_shape=jax.ShapeDtypeStruct((2, GROUP, rows, 2 * HD), jnp.bfloat16),
        in_specs=[in_vmem()] * 7,
        out_specs=in_vmem(),
        scratch_shapes=[
            pltpu.VMEM((rows, projector.shape[0]), jnp.bfloat16),
            pltpu.VMEM((rows, own.shape[1]), jnp.float32),
        ],
        compiler_params=params(),
    )(*pieces, projector, own, other)


def rope_tables(positions):
    inverse = 500000.0 ** (-np.arange(HD // 2) * (2.0 / HD))
    angles = np.arange(positions)[:, None] * inverse[None, :]
    cosine, sine = np.cos(angles), np.sin(angles)
    return (
        np.concatenate([cosine, cosine], axis=1).astype(np.float32),
        np.concatenate([-sine, sine], axis=1).astype(np.float32),
    )


def paired_body(
    text_states,
    vision_states,
    visible_tiles,
    vision_norm_gain,
    vision_fc1,
    vision_fc2,
    vision_gate,
    projector,
    cross_norm,
    cross_q,
    cross_kv,
    cross_qk_gain,
    cross_o,
    cross_gate,
    self_norm,
    self_q,
    self_kv,
    self_o,
):
    core = lax.axis_index("section")
    chip = lax.axis_index("tp")
    seq_len, local_width = text_states.shape
    rows = seq_len // 2
    full_width = local_width * lax.axis_size("tp")
    member = jnp.where(core == 0, chip % GROUP, chip // GROUP)

    after = lax.optimization_barrier
    own_cross_kv, own_cross_q, own_cross_o = cross_kv[0], cross_q[0], cross_o[0]
    own_self_kv, own_self_q, own_self_o = self_kv[0], self_q[0], self_o[0]

    hidden = lax.dynamic_slice_in_dim(text_states, core * rows, rows, 0)
    entry = jnp.concatenate(
        [hidden, cross_norm, self_norm, jnp.zeros((14, local_width), jnp.bfloat16)]
    )
    text_come = send_group([entry] * GROUP, (GROUP, GROUP))
    branch = encoder_part(vision_states, vision_norm_gain[None], vision_fc1.T, vision_fc2)
    come = send_group(branch, (1, GROUP))
    come, text_come, own, self_norm, cross_qk_gain, cross_gate = after(
        (come, text_come, own_cross_kv, self_norm, cross_qk_gain, cross_gate)
    )
    near = total([branch[0]] + come).astype(jnp.bfloat16)
    come = send_group([near] * GROUP, (GROUP, 1))
    far_cross_kv = swap_cores(own)
    small = jnp.concatenate(
        [
            self_norm.astype(jnp.float32),
            jnp.pad(cross_qk_gain.reshape(1, -1), ((0, 0), (0, local_width - 2 * HD))),
            jnp.broadcast_to(cross_gate[None], (1, local_width)),
        ]
    )
    far_small = swap_cores(small)
    text = jnp.stack([entry] + text_come)
    come, far_cross_kv, far_small, text, own = after(
        (come, far_cross_kv, far_small, text, own_cross_q)
    )
    branch_rows = total([near] + come)
    vis_rows = lax.dynamic_index_in_dim(
        vision_states.reshape(branch.shape), member, 0, keepdims=False
    )
    vis_out = (vis_rows.astype(jnp.float32) + jnp.tanh(vision_gate[0]) * branch_rows).astype(
        jnp.bfloat16
    )
    come = send_group([vis_out] * GROUP, (1, GROUP))
    text_come = send_xor(text, (1, 2))
    far_cross_q = swap_cores(own)
    come, text_come, far_cross_q, own = after((come, text_come, far_cross_q, own_cross_o))
    scalars = [jnp.where(core == 0, small, far_small), jnp.where(core == 0, far_small, small)]

    image_parts = image_part([vis_out] + come, projector, own_cross_kv, far_cross_kv)
    come = send_group(image_parts[0], (GROUP, GROUP))
    text = jnp.concatenate([text, text_come])
    text_come = send_xor(text, (2, 1))
    far_cross_o = swap_cores(own)
    come, text_come, far_cross_o, own = after((come, text_come, far_cross_o, own_self_kv))
    near = total([image_parts[0, 0]] + come).astype(jnp.bfloat16)
    come = send_group([near] * GROUP, (1, 1))
    gains = jnp.concatenate([text[:, rows:], text_come[:, rows:]])
    far_gains = swap_cores(gains)
    far_self_kv = swap_cores(own)
    gains = (gains, far_gains)
    text = [half[at : at + GROUP] for half in (text, text_come) for at in (0, GROUP)]
    queries = plain_query_part(0, 0, rows, text, gains, (own_cross_q, far_cross_q))
    come, queries, far_self_kv = after((come, queries, far_self_kv))
    parts = [near] + come

    def image_rows(kv_rows, section):
        key_gain = scalars[section][1, HD : 2 * HD]
        near = jnp.concatenate(
            [rms_norm(kv_rows[:, :HD], key_gain), kv_rows[:, HD:]], axis=1
        ).astype(jnp.bfloat16)
        return near, swap_cores(near)

    near, far = image_rows(total(parts), 0)
    tile_rows = 2 * vision_states.shape[0] // TILES
    tiles = jnp.broadcast_to(visible_tiles[:, None], (seq_len, HD))
    cosine, sine = (jnp.asarray(table) for table in rope_tables(seq_len))

    def self_block(section, hidden, beside_mixed):
        nonlocal far_self_o
        steps = head_steps(key_value_part(section, hidden, scalars[section], own_self_kv, far_self_kv))
        come = send_group([hidden] * GROUP, (GROUP, 1))
        kv_rows = steps[1](steps[0]())
        extra = steps[2](kv_rows)
        if section == 0:
            far_self_o = swap_cores(after((own_self_o, hidden))[0])
            come, kv_rows, extra, far_self_o = after((come, kv_rows, extra, far_self_o))
        else:
            come, kv_rows, extra = after((come, kv_rows, extra))
        first = jnp.stack([hidden] + come)
        come = send_group([first] * GROUP, (1, GROUP))
        kv_rows = steps[3](kv_rows, extra)
        kv_rows = steps[5](kv_rows, steps[4](kv_rows))
        come, kv_rows, extra = after((come, kv_rows, steps[6](kv_rows)))
        near = steps[7](kv_rows, extra).astype(jnp.bfloat16)
        far = swap_cores(near)
        queries = query_part(
            section, 1, rows, [first] + come, gains, (own_self_q, far_self_q), cosine, sine
        )
        mixed = self_mix(full_width, queries, near, far, cosine, sine)
        pieces, extras = gather_chips(mixed, *beside_mixed)
        hidden = out_part(
            section, False, pieces, hidden, scalars[section], tiles, own_self_o, far_self_o
        )
        return hidden, extras

    mixed = cross_mix_from(tile_rows, queries, near, far, tiles, scalars[0])
    mixed, own, second_kept = after((mixed, own_self_q, image_parts[1]))
    second = head_steps(second_kept)
    pieces, ((far_self_q, come), second_come) = gather_chips(
        mixed,
        lambda: (swap_cores(own), second[0]()),
        lambda extra: second[2](second[1](extra[1])),
    )
    second_rows = second[3](second[1](come), second_come)
    hidden = out_part(0, True, pieces, hidden, scalars[0], tiles, own_cross_o, far_cross_o)
    far_self_o = None
    hidden, (come, second_come) = self_block(
        0,
        hidden,
        (lambda: second[4](second_rows), lambda extra: second[6](second[5](second_rows, extra))),
    )
    second_rows = second[7](second[5](second_rows, come), second_come)
    results = [hidden]
    near, far = image_rows(second_rows, 1)
    pieces, (far,) = gather_chips(hidden, lambda: far)
    mixed = cross_mix(
        1, 0, tile_rows, rows, pieces, gains, (own_cross_q, far_cross_q), near, far, tiles, scalars[1]
    )
    pieces, _ = gather_chips(mixed)
    hidden = out_part(1, True, pieces, hidden, scalars[1], tiles, own_cross_o, far_cross_o)
    hidden, _ = self_block(1, hidden, ())
    results.append(hidden)
    come = swap_cores(jnp.where(core == 0, results[1], results[0]))
    return jnp.where(
        core == 0,
        jnp.concatenate([results[0], come], axis=0),
        jnp.concatenate([come, results[1]], axis=0),
    )[None]


def solution(mesh):
    chips = mesh.shape["tp"]
    paired = mesh.shape["section"] == 2 and chips == GROUP * GROUP and HEADS == 2 * chips
    body = paired_body if paired else blocked_body
    in_specs = (
        P(None, "tp"),
        P("section", None),
        P(),
        P(),
        P(None, "tp"),
        P("tp", None),
        P(),
        P(None, "tp"),
        P("section", "tp"),
        P("section", None, "tp"),
        P("section", "tp", None),
        P("section", None, None),
        P("section", None, "tp"),
        P("section"),
        P("section", "tp"),
        P("section", None, "tp"),
        P("section", "tp", None),
        P("section", None, "tp"),
    )
    out_specs = P("section", None, "tp")
    return jax.shard_map(body, mesh=mesh, in_specs=in_specs, out_specs=out_specs, check_vma=False)
```

```python
import functools

import jax
import jax.numpy as jnp
import numpy as np
from jax import lax
from jax.experimental import pallas as pl
from jax.experimental.pallas import tpu as pltpu
from jax.sharding import PartitionSpec as P

HD = 128
HEADS = 32
KV = 4
TILES = 4
ROWS = 64
BLOCKS = 2


epsilon = 1e-05


def from_behind(block, axis, distance):
    devices = range(lax.axis_size(axis))
    route = [(i - distance, i) for i in devices if i - distance in devices]
    return lax.ppermute(block, axis, route)


def rms_norm(values, gain_row):
    mean_square = jnp.mean(values * values, axis=-1, keepdims=True)
    return values * lax.rsqrt(mean_square + epsilon) * gain_row.astype(jnp.float32)


def rotate(values, positions):
    half_dim = values.shape[-1] // 2
    exponents = jnp.arange(half_dim, dtype=jnp.float32) * (2.0 / values.shape[-1])
    inverse = jnp.float32(500000.0) ** (-exponents)
    angles = positions.astype(jnp.float32)[:, None] * inverse[None, :]
    cosine = jnp.cos(angles)[:, None, :]
    sine = jnp.sin(angles)[:, None, :]
    lower = values[..., :half_dim]
    upper = values[..., half_dim:]
    return jnp.concatenate([lower * cosine - upper * sine, upper * cosine + lower * sine], axis=-1)


def softmax_rows(scores):
    top_score = jnp.max(scores, axis=-1, keepdims=True)
    raised = jnp.exp(scores - top_score)
    return raised / jnp.sum(raised, axis=-1, keepdims=True)


def head_columns(kv_rows, kv_head):
    key_part = lax.dynamic_slice_in_dim(kv_rows, kv_head * HD, HD, 1)
    value_part = lax.dynamic_slice_in_dim(kv_rows, (KV + kv_head) * HD, HD, 1)
    return (key_part, value_part)


def attend_one(queries, key_rows, value_rows, allowed):
    scores = jnp.einsum(
        "rhd,jd->hrj", queries, key_rows, preferred_element_type=jnp.float32
    ) * HD ** (-0.5)
    scores = jnp.where(allowed[None], scores, -1e30)
    weights = softmax_rows(scores).astype(jnp.bfloat16)
    mixed_heads = jnp.einsum("hrj,jd->rhd", weights, value_rows, preferred_element_type=jnp.float32)
    return mixed_heads.astype(jnp.bfloat16).reshape(queries.shape[0], -1)


def out_fold(weight, segment):
    return jnp.dot(segment, weight, preferred_element_type=jnp.float32)


def blocked_body(
    text_states,
    vision_states,
    visible_tiles,
    vision_norm_gain,
    vision_fc1,
    vision_fc2,
    vision_gate,
    projector,
    cross_norm,
    cross_q,
    cross_kv,
    cross_qk_gain,
    cross_o,
    cross_gate,
    self_norm,
    self_q,
    self_kv,
    self_o,
):
    section_idx = lax.axis_index("section")
    section_total = lax.axis_size("section")
    tp_index = lax.axis_index("tp")
    local_width = text_states.shape[1]
    heads_local = cross_q.shape[2] // HD
    kv_group = HEADS // KV
    kv_head = tp_index * heads_local // kv_group
    vis_f32 = vision_states.astype(jnp.float32)
    centre = jnp.mean(vis_f32, axis=-1, keepdims=True)
    spread = jnp.mean((vis_f32 - centre) ** 2, axis=-1, keepdims=True)
    normed_vis = ((vis_f32 - centre) * lax.rsqrt(spread + epsilon) * vision_norm_gain).astype(
        jnp.bfloat16
    )
    vis_hidden = jax.nn.gelu(
        jnp.dot(normed_vis, vision_fc1, preferred_element_type=jnp.float32), approximate=False
    ).astype(jnp.bfloat16)
    vis_branch = lax.psum(jnp.dot(vis_hidden, vision_fc2, preferred_element_type=jnp.float32), "tp")
    vis_out = (vis_f32 + jnp.tanh(vision_gate[0]) * vis_branch).astype(jnp.bfloat16)
    every_row = lax.all_gather(vis_out, "section", axis=0, tiled=True)
    image_feats = jnp.dot(every_row, projector, preferred_element_type=jnp.float32).astype(
        jnp.bfloat16
    )
    image_count = image_feats.shape[0]
    kv_term = jnp.dot(image_feats, cross_kv[0], preferred_element_type=jnp.float32)
    key_gain = cross_qk_gain[0, 1]
    kv_image = lax.psum(kv_term, "tp")
    key_part, value_part = head_columns(kv_image, kv_head)
    key_img = rms_norm(key_part, key_gain).astype(jnp.bfloat16)
    val_img = value_part.astype(jnp.bfloat16)
    tile_of = jnp.arange(image_count, dtype=jnp.int32) // (image_count // TILES)
    seq_len = text_states.shape[0]
    positions_all = jnp.arange(seq_len, dtype=jnp.int32)
    gate_cross = jnp.tanh(cross_gate[0])
    key_cache = jnp.zeros((seq_len, HD), jnp.bfloat16)
    val_cache = jnp.zeros((seq_len, HD), jnp.bfloat16)
    outputs = jnp.zeros((seq_len, local_width), jnp.bfloat16)
    incoming = jnp.zeros((ROWS, local_width), jnp.bfloat16)
    step_count = BLOCKS + section_total - 1
    for step_no in range(step_count):
        block_idx = step_no - section_idx
        is_live = (block_idx >= 0) & (block_idx < BLOCKS)
        row_start = jnp.clip(block_idx, 0, BLOCKS - 1) * ROWS
        entry_block = min(step_no, BLOCKS - 1)
        first_rows = text_states[entry_block * ROWS : (entry_block + 1) * ROWS]
        current = jnp.where(section_idx == 0, first_rows, incoming)
        positions = row_start + jnp.arange(ROWS, dtype=jnp.int32)
        whole_rows, gain_row = (
            lax.all_gather(current, "tp", axis=1, tiled=True),
            lax.all_gather(cross_norm, "tp", axis=1, tiled=True),
        )
        normed = rms_norm(whole_rows.astype(jnp.float32), gain_row[0]).astype(jnp.bfloat16)
        queries = jnp.dot(normed, cross_q[0], preferred_element_type=jnp.float32).reshape(
            ROWS, heads_local, HD
        )
        queries = rms_norm(queries, cross_qk_gain[0, 0]).astype(jnp.bfloat16)
        row_tiles = lax.dynamic_slice_in_dim(visible_tiles, row_start, ROWS)
        allowed = tile_of[None, :] < row_tiles[:, None]
        mixed_heads = attend_one(queries, key_img, val_img, allowed)
        cross_branch = out_fold(cross_o[0], lax.all_gather(mixed_heads, "tp", axis=1, tiled=True))
        cross_branch = cross_branch * (row_tiles > 0).astype(jnp.float32)[:, None]
        current = (current.astype(jnp.float32) + gate_cross * cross_branch).astype(jnp.bfloat16)
        whole_rows, gain_row = (
            lax.all_gather(current, "tp", axis=1, tiled=True),
            lax.all_gather(self_norm, "tp", axis=1, tiled=True),
        )
        normed = rms_norm(whole_rows.astype(jnp.float32), gain_row[0]).astype(jnp.bfloat16)
        queries = rotate(
            jnp.dot(normed, self_q[0], preferred_element_type=jnp.float32).reshape(
                ROWS, heads_local, HD
            ),
            positions,
        ).astype(jnp.bfloat16)
        own_cols = lax.dynamic_slice_in_dim(normed, tp_index * local_width, local_width, 1)
        kv_text = lax.psum(
            jnp.dot(own_cols, self_kv[0], preferred_element_type=jnp.float32).astype(jnp.bfloat16),
            "tp",
        ).astype(jnp.float32)
        key_part, value_part = head_columns(kv_text, kv_head)
        new_keys = rotate(key_part[:, None, :], positions)[:, 0].astype(jnp.bfloat16)
        new_vals = value_part.astype(jnp.bfloat16)
        key_cache = jnp.where(
            is_live, lax.dynamic_update_slice_in_dim(key_cache, new_keys, row_start, 0), key_cache
        )
        val_cache = jnp.where(
            is_live, lax.dynamic_update_slice_in_dim(val_cache, new_vals, row_start, 0), val_cache
        )
        causal = positions_all[None, :] <= positions[:, None]
        mixed_heads = attend_one(queries, key_cache, val_cache, causal)
        self_branch = out_fold(self_o[0], lax.all_gather(mixed_heads, "tp", axis=1, tiled=True))
        current = (current.astype(jnp.float32) + self_branch).astype(jnp.bfloat16)
        outputs = jnp.where(
            is_live, lax.dynamic_update_slice_in_dim(outputs, current, row_start, 0), outputs
        )
        if step_no + 1 < step_count:
            incoming = from_behind(current, "section", 1)
    return outputs[None]


VMEM_LIMIT = 11 * 1024 * 1024
GROUP = 4


def params(limit=VMEM_LIMIT):
    return pltpu.CompilerParams(vmem_limit_bytes=limit)


def in_vmem():
    return pl.BlockSpec(memory_space=pltpu.VMEM)


def swap_cores(block):
    return lax.ppermute(block, "section", [(0, 1), (1, 0)])


def send_xor(block, masks):
    chips = lax.axis_size("tp")
    route = [
        (core * chips + chip, core * chips + (chip ^ masks[core]))
        for core in range(2)
        for chip in range(chips)
    ]
    return lax.ppermute(block, ("section", "tp"), route)


def send_group(blocks, scale):
    order = range(GROUP - 1, 0, -1)
    sent = {k: send_xor(blocks[k], (scale[0] * k, scale[1] * k)) for k in order}
    return [sent[k] for k in range(1, GROUP)]


def gather_chips(block, beside=None):
    extra = beside() if beside is not None else ()
    come = send_group([block] * GROUP, (GROUP, 1))
    first = jnp.stack([block] + come)
    come = send_group([first] * GROUP, (1, GROUP))
    come, extra = lax.optimization_barrier((come, extra))
    return [first] + come, extra


def total(parts):
    return sum((part.astype(jnp.float32) for part in parts[1:]), parts[0].astype(jnp.float32))


def head_steps(blocks):
    def fold(kept, come):
        return (kept.astype(jnp.float32) + come.astype(jnp.float32)).astype(jnp.bfloat16)

    return [
        lambda: send_xor(blocks[2:], (2 * GROUP, 2 * GROUP)),
        lambda come: fold(blocks[:2], come),
        lambda rows: send_xor(rows[1], (GROUP, GROUP)),
        lambda rows, come: fold(rows[0], come),
        lambda rows: send_xor(rows, (1, 1)),
        lambda rows, come: fold(rows, come),
        lambda rows: send_xor(rows, (2, 2)),
        lambda rows, come: rows.astype(jnp.float32) + come.astype(jnp.float32),
    ]


def gather_mask(core, at):
    outer, inner = divmod(at, GROUP)
    return outer ^ GROUP * inner if core == 0 else inner ^ GROUP * outer


def text_mask(core, at):
    outer, inner = divmod(at, GROUP)
    return (outer if core == 0 else outer % 2 * 2 + outer // 2) ^ GROUP * inner


def with_weight(section, own, other, run):
    core = lax.axis_index("section")

    @pl.when(core == section)
    def _():
        run(section, *own)

    @pl.when(core != section)
    def _():
        run(1 - section, *other)


def weight_rows(weight_ref, mask, rows):
    source = lax.axis_index("tp") ^ mask
    return weight_ref[pl.ds(pl.multiple_of(source * rows, rows), rows), :]


def project(section, gain_at, rows, x_refs, gain_refs, weight_refs, product_ref, mask_of=gather_mask):
    depth = x_refs[0].shape[2]
    pieces = range(GROUP * GROUP)
    gain_place = {text_mask(section, at): at for at in pieces}

    def run(core, gain_ref, weight_ref):
        product = jnp.zeros(product_ref.shape, jnp.float32)
        squares = jnp.zeros((rows, depth), jnp.float32)
        for at in pieces:
            mask = mask_of(core, at)
            piece = x_refs[at // GROUP][at % GROUP, :rows, :].astype(jnp.float32)
            squares = squares + piece * piece
            gain_row = gain_ref[gain_place[mask], gain_at : gain_at + 1, :].astype(jnp.float32)
            scaled = (piece * gain_row).astype(jnp.bfloat16)
            product = product + jnp.dot(
                scaled, weight_rows(weight_ref, mask, depth), preferred_element_type=jnp.float32
            )
        mean_square = jnp.sum(squares, axis=1, keepdims=True) / (GROUP * GROUP * depth)
        product_ref[...] = product * lax.rsqrt(mean_square + epsilon)

    with_weight(
        section, (gain_refs[0], weight_refs[0]), (gain_refs[1], weight_refs[1]), run
    )
    return product_ref[...]


def dot_rows(left, right):
    return lax.dot_general(
        left, right, (((1,), (1,)), ((), ())), preferred_element_type=jnp.float32
    )


def mix(queries, key_sets, value_sets, allowed_sets, value_scales):
    scores = []
    for keys, allowed, scale in zip(key_sets, allowed_sets, value_scales):
        part = dot_rows(queries, keys) * HD ** (-0.5)
        if scale is not None:
            part = part * scale
        scores.append(jnp.where(allowed, part, -1e30))
    top = functools.reduce(
        jnp.maximum, [jnp.max(part, axis=1, keepdims=True) for part in scores]
    )
    raised = [jnp.exp(part - top) for part in scores]
    bottom = sum(jnp.sum(part, axis=1, keepdims=True) for part in raised)
    mixed = jnp.zeros(queries.shape, jnp.float32)
    for part, values, scale in zip(raised, value_sets, value_scales):
        weights = part / bottom
        if scale is not None:
            weights = weights * scale
        mixed = mixed + jnp.dot(
            weights.astype(jnp.bfloat16), values, preferred_element_type=jnp.float32
        )
    return mixed.astype(jnp.bfloat16)


def by_head(queries):
    heads = queries.shape[1] // HD
    return jnp.concatenate([queries[:, h * HD : (h + 1) * HD] for h in range(heads)], axis=0)


def side_by_side(mixed, rows):
    return jnp.concatenate(
        [mixed[start : start + rows] for start in range(0, mixed.shape[0], rows)], axis=1
    )


def cross_attend(tile_rows, queries, near_ref, far_ref, tiles_ref, qk_ref, out_ref):
    core = lax.axis_index("section")
    rows = out_ref.shape[0]
    queries = rms_norm(by_head(queries), qk_ref[1:2, :HD]).astype(jnp.bfloat16)
    row_tiles = tiles_ref[pl.ds(pl.multiple_of(core * rows, rows), rows), :]
    row_tiles = jnp.concatenate([row_tiles] * (queries.shape[0] // rows), axis=0)
    count = near_ref.shape[0]
    key_at = lax.broadcasted_iota(jnp.int32, (queries.shape[0], count), 1)
    allowed = [
        key_at + core * count < row_tiles * tile_rows,
        key_at + (1 - core) * count < row_tiles * tile_rows,
    ]
    sets = (near_ref[...], far_ref[...])
    mixed = mix(
        queries, [kv[:, :HD] for kv in sets], [kv[:, HD:] for kv in sets], allowed, (None, None)
    )
    out_ref[...] = side_by_side(mixed, rows)


def attend_kernel(tile_rows, q_ref, near_ref, far_ref, tiles_ref, qk_ref, out_ref):
    cross_attend(tile_rows, q_ref[...], near_ref, far_ref, tiles_ref, qk_ref, out_ref)


def cross_mix(tile_rows, queries, near, far, tiles, qk):
    return pl.pallas_call(
        functools.partial(attend_kernel, tile_rows),
        out_shape=jax.ShapeDtypeStruct(queries.shape, jnp.bfloat16),
        in_specs=[in_vmem()] * 5,
        out_specs=in_vmem(),
        compiler_params=params(),
    )(queries, near, far, tiles, qk)


def plain_query_kernel(section, gain_at, mask_of, *refs):
    x_refs, gain_refs, weight_refs, out_ref = refs[:-5], refs[-5:-3], refs[-3:-1], refs[-1]
    rows = out_ref.shape[0]
    project(section, gain_at, rows, x_refs, gain_refs, weight_refs, out_ref, mask_of)


def plain_query_part(section, gain_at, rows, pieces, gains, weights, mask_of=gather_mask):
    return pl.pallas_call(
        functools.partial(plain_query_kernel, section, gain_at, mask_of),
        out_shape=jax.ShapeDtypeStruct((rows, weights[0].shape[1]), jnp.float32),
        in_specs=[in_vmem()] * (len(pieces) + 4),
        out_specs=in_vmem(),
        compiler_params=params(),
    )(*pieces, *gains, *weights)


def turn(values, cosine, sine):
    half = HD // 2
    swapped = jnp.concatenate([values[:, half:], values[:, :half]], axis=1)
    return values * cosine + swapped * sine


def query_kernel(section, gain_at, *refs):
    x_refs, gain_refs, weight_refs = refs[:GROUP], refs[GROUP : GROUP + 2], refs[GROUP + 2 : GROUP + 4]
    cosine_ref, sine_ref, out_ref, product_ref = refs[GROUP + 4 :]
    rows = product_ref.shape[0]
    core = lax.axis_index("section")
    mine = pl.ds(pl.multiple_of(core * rows, rows), rows)
    queries = project(section, gain_at, rows, x_refs, gain_refs, weight_refs, product_ref)
    for head in range(queries.shape[1] // HD):
        turned = turn(queries[:, head * HD : (head + 1) * HD], cosine_ref[mine, :], sine_ref[mine, :])
        out_ref[head * rows : (head + 1) * rows, :] = turned.astype(jnp.bfloat16)


def query_part(section, gain_at, rows, pieces, gains, weights, cosine, sine):
    columns = weights[0].shape[1]
    return pl.pallas_call(
        functools.partial(query_kernel, section, gain_at),
        out_shape=jax.ShapeDtypeStruct((rows * columns // HD, HD), jnp.bfloat16),
        in_specs=[in_vmem()] * (GROUP + 6),
        out_specs=in_vmem(),
        scratch_shapes=[pltpu.VMEM((rows, columns), jnp.float32)],
        compiler_params=params(),
    )(*pieces, *gains, *weights, cosine, sine)


def self_kernel(width, q_ref, near_ref, far_ref, cosine_ref, sine_ref, out_ref):
    core = lax.axis_index("section")
    rows = out_ref.shape[0]
    queries = q_ref[...]
    shape = (queries.shape[0], rows)
    row_at = lax.rem(lax.broadcasted_iota(jnp.int32, shape, 0), rows) + core * rows
    key_at = lax.broadcasted_iota(jnp.int32, shape, 1)
    keys, values, allowed, scales = [], [], [], []
    for ref, side in ((near_ref, core), (far_ref, 1 - core)):
        at = pl.ds(pl.multiple_of(side * rows, rows), rows)
        raw = ref[:rows, :HD].astype(jnp.float32)
        keys.append(turn(raw, cosine_ref[at, :], sine_ref[at, :]).astype(jnp.bfloat16))
        values.append(ref[:rows, HD:])
        allowed.append(key_at + side * rows <= row_at)
        square_sum = ref[rows : rows + 1, :rows].astype(jnp.float32)
        scales.append(lax.rsqrt(square_sum / width + epsilon))
    out_ref[...] = side_by_side(mix(queries, keys, values, allowed, scales), rows)


def self_mix(width, queries, near, far, cosine, sine):
    rows = cosine.shape[0] // 2
    return pl.pallas_call(
        functools.partial(self_kernel, width),
        out_shape=jax.ShapeDtypeStruct((rows, queries.shape[0] // rows * HD), jnp.bfloat16),
        in_specs=[in_vmem()] * 5,
        out_specs=in_vmem(),
        compiler_params=params(),
    )(queries, near, far, cosine, sine)


def key_value_kernel(section, hidden_ref, small_ref, own_ref, other_ref, out_ref, product):
    high = lax.axis_index("tp") // GROUP
    rows = hidden_ref.shape[0]
    hidden = hidden_ref[...].astype(jnp.float32)
    scaled = (hidden * small_ref[0:1, :]).astype(jnp.bfloat16)
    squares = hidden * hidden
    top = squares.astype(jnp.bfloat16)
    rest = (squares - top.astype(jnp.float32)).astype(jnp.bfloat16)
    ones = jnp.ones((16, hidden.shape[1]), jnp.bfloat16)
    square_sum = dot_rows(ones, top) + dot_rows(ones, rest)
    square_sum = jnp.concatenate(
        [square_sum, jnp.zeros((16, 2 * HD - rows), jnp.float32)], axis=1
    ).astype(jnp.bfloat16)

    def run(core, weight_ref):
        product[...] = jnp.dot(scaled, weight_ref[...], preferred_element_type=jnp.float32)

    with_weight(section, (own_ref,), (other_ref,), run)
    for k in range(GROUP):
        for part in range(2):
            start = pl.multiple_of((part * KV + (high ^ k)) * HD, HD)
            out_ref[k, :rows, part * HD : (part + 1) * HD] = product[:, pl.ds(start, HD)].astype(
                jnp.bfloat16
            )
        out_ref[k, rows:, :] = square_sum


def key_value_part(section, hidden, small, own, other):
    rows = hidden.shape[0]
    return pl.pallas_call(
        functools.partial(key_value_kernel, section),
        out_shape=jax.ShapeDtypeStruct((GROUP, rows + 16, 2 * HD), jnp.bfloat16),
        in_specs=[in_vmem()] * 4,
        out_specs=in_vmem(),
        scratch_shapes=[pltpu.VMEM((rows, own.shape[1]), jnp.float32)],
        compiler_params=params(),
    )(hidden, small, own, other)


def out_kernel(section, gated, *refs):
    x_refs = refs[:GROUP]
    hidden_ref, small_ref, tiles_ref, own_ref, other_ref, out_ref = refs[GROUP:]
    rows = out_ref.shape[0]
    depth = x_refs[0].shape[2]

    def run(core, weight_ref):
        branch = jnp.zeros(out_ref.shape, jnp.float32)
        for at in range(GROUP * GROUP):
            branch = branch + jnp.dot(
                x_refs[at // GROUP][at % GROUP],
                weight_rows(weight_ref, gather_mask(core, at), depth),
                preferred_element_type=jnp.float32,
            )
        if gated:
            row_tiles = tiles_ref[core * rows : (core + 1) * rows, :1]
            branch = branch * (row_tiles > 0).astype(jnp.float32) * jnp.tanh(small_ref[2:3, :])
        out_ref[...] = (hidden_ref[...].astype(jnp.float32) + branch).astype(jnp.bfloat16)

    with_weight(section, (own_ref,), (other_ref,), run)


def out_part(section, gated, pieces, hidden, small, tiles, own, other):
    return pl.pallas_call(
        functools.partial(out_kernel, section, gated),
        out_shape=jax.ShapeDtypeStruct(hidden.shape, jnp.bfloat16),
        in_specs=[in_vmem()] * (GROUP + 5),
        out_specs=in_vmem(),
        compiler_params=params(),
    )(*pieces, hidden, small, tiles, own, other)


def encoder_kernel(states_hbm, gain_ref, fc1_hbm, fc2_hbm, norm_ref, qk_ref, gate_ref, *refs):
    out_refs, small_ref = refs[:GROUP], refs[GROUP]
    states_ref, fc1_ref, fc2_ref, product, sems = refs[GROUP + 1 :]
    copies = [
        pltpu.make_async_copy(source, target, sems.at[at])
        for at, (source, target) in enumerate(
            ((states_hbm, states_ref), (fc1_hbm, fc1_ref), (fc2_hbm, fc2_ref))
        )
    ]
    for copy in copies:
        copy.start()
    core = lax.axis_index("section")
    chip = lax.axis_index("tp")
    member = jnp.where(core == 0, chip % GROUP, chip // GROUP)
    small_ref[0:1, :] = norm_ref[...].astype(jnp.float32)
    small_ref[1:2, :] = jnp.concatenate(
        [qk_ref[0:1, :], qk_ref[1:2, :], jnp.zeros((1, norm_ref.shape[1] - 2 * HD), jnp.float32)],
        axis=1,
    )
    small_ref[2:3, :] = jnp.full((1, norm_ref.shape[1]), gate_ref[0], jnp.float32)
    copies[0].wait()
    states = states_ref[...].astype(jnp.float32)
    centred = states - jnp.mean(states, axis=-1, keepdims=True)
    spread = jnp.mean(centred * centred, axis=-1, keepdims=True)
    normed = (centred * lax.rsqrt(spread + epsilon) * gain_ref[...][None]).astype(jnp.bfloat16)
    copies[1].wait()
    inner = dot_rows(normed, fc1_ref[...])
    inner = (0.5 * inner * (1.0 + lax.erf(inner * 2.0 ** (-0.5)))).astype(jnp.bfloat16)
    copies[2].wait()
    product[...] = jnp.dot(inner, fc2_ref[...], preferred_element_type=jnp.float32).astype(
        jnp.bfloat16
    )
    rows = out_refs[0].shape[0]
    for k in range(GROUP):
        out_refs[k][...] = product[pl.ds(pl.multiple_of((member ^ k) * rows, rows), rows), :]


def encoder_part(states, gain, fc1, fc2, norm, qk, gate):
    rows, width = states.shape
    in_place = pl.BlockSpec(memory_space=pltpu.HBM)
    return pl.pallas_call(
        encoder_kernel,
        out_shape=[jax.ShapeDtypeStruct((rows // GROUP, width), jnp.bfloat16)] * GROUP
        + [jax.ShapeDtypeStruct((3, norm.shape[1]), jnp.float32)],
        in_specs=[in_place, in_vmem(), in_place, in_place, in_vmem(), in_vmem()]
        + [pl.BlockSpec(memory_space=pltpu.SMEM)],
        out_specs=[in_vmem()] * (GROUP + 1),
        scratch_shapes=[
            pltpu.VMEM(states.shape, jnp.bfloat16),
            pltpu.VMEM(fc1.shape, jnp.bfloat16),
            pltpu.VMEM(fc2.shape, jnp.bfloat16),
            pltpu.VMEM((rows, width), jnp.bfloat16),
            pltpu.SemaphoreType.DMA((3,)),
        ],
        compiler_params=params(5 * VMEM_LIMIT),
    )(states, gain, fc1, fc2, norm, qk, gate)


def image_kernel(p0, p1, p2, p3, projector_ref, own_ref, other_ref, _, out_ref, rows_ref, kv_ref):
    core = lax.axis_index("section")
    chip = lax.axis_index("tp")
    low, high = chip % GROUP, chip // GROUP
    member = jnp.where(core == 0, low, high)
    count = p0.shape[0]
    for k, ref in enumerate((p0, p1, p2, p3)):
        rows_ref[pl.ds(pl.multiple_of((member ^ k) * count, count), count), :] = ref[...]
    feats = jnp.dot(
        rows_ref[...], projector_ref[...], preferred_element_type=jnp.float32
    ).astype(jnp.bfloat16)
    for section in range(2):
        weight = jnp.where(core == section, own_ref[...], other_ref[...])
        kv_ref[...] = jnp.dot(feats, weight, preferred_element_type=jnp.float32)
        for k in range(GROUP):
            head = high ^ k
            for part in range(2):
                start = pl.multiple_of((part * KV + head) * HD, HD)
                out_ref[section, k, :, part * HD : (part + 1) * HD] = kv_ref[
                    :, pl.ds(start, HD)
                ].astype(jnp.bfloat16)


def image_part(pieces, projector, own, other, begun):
    rows = GROUP * pieces[0].shape[0]
    return pl.pallas_call(
        image_kernel,
        out_shape=jax.ShapeDtypeStruct((2, GROUP, rows, 2 * HD), jnp.bfloat16),
        in_specs=[in_vmem()] * 8,
        out_specs=in_vmem(),
        scratch_shapes=[
            pltpu.VMEM((rows, projector.shape[0]), jnp.bfloat16),
            pltpu.VMEM((rows, own.shape[1]), jnp.float32),
        ],
        compiler_params=params(),
    )(*pieces, projector, own, other, begun)


def rope_tables(positions):
    inverse = 500000.0 ** (-np.arange(HD // 2) * (2.0 / HD))
    angles = np.arange(positions)[:, None] * inverse[None, :]
    cosine, sine = np.cos(angles), np.sin(angles)
    return (
        np.concatenate([cosine, cosine], axis=1).astype(np.float32),
        np.concatenate([-sine, sine], axis=1).astype(np.float32),
    )


def paired_body(
    text_states,
    vision_states,
    visible_tiles,
    vision_norm_gain,
    vision_fc1,
    vision_fc2,
    vision_gate,
    projector,
    cross_norm,
    cross_q,
    cross_kv,
    cross_qk_gain,
    cross_o,
    cross_gate,
    self_norm,
    self_q,
    self_kv,
    self_o,
):
    core = lax.axis_index("section")
    chip = lax.axis_index("tp")
    seq_len, local_width = text_states.shape
    rows = seq_len // 2
    full_width = local_width * lax.axis_size("tp")
    member = jnp.where(core == 0, chip % GROUP, chip // GROUP)

    after = lax.optimization_barrier
    own_cross_kv, own_cross_q, own_cross_o = cross_kv[0], cross_q[0], cross_o[0]
    own_self_kv, own_self_q, own_self_o = self_kv[0], self_q[0], self_o[0]

    hidden = lax.dynamic_slice_in_dim(text_states, core * rows, rows, 0)
    entry = jnp.concatenate(
        [hidden, cross_norm, self_norm, jnp.zeros((14, local_width), jnp.bfloat16)]
    )
    text_come = send_group([entry] * GROUP, (GROUP, GROUP))
    *branch, small = encoder_part(
        vision_states, vision_norm_gain, vision_fc1.T, vision_fc2, self_norm, cross_qk_gain[0], cross_gate
    )
    come = send_group(branch, (1, GROUP))
    come, text_come, own, small = after((come, text_come, own_cross_kv, small))
    near = total([branch[0]] + come).astype(jnp.bfloat16)
    come = send_group([near] * GROUP, (GROUP, 1))
    far_cross_kv = swap_cores(own)
    far_small = swap_cores(small)
    text = jnp.stack([entry] + text_come)
    come, far_small, text, own, begun = after(
        (come, far_small, text, own_cross_q, far_cross_kv[:16, :HD])
    )
    branch_rows = total([near] + come)
    vis_rows = lax.dynamic_index_in_dim(
        vision_states.reshape((GROUP,) + branch[0].shape), member, 0, keepdims=False
    )
    vis_out = (vis_rows.astype(jnp.float32) + jnp.tanh(vision_gate[0]) * branch_rows).astype(
        jnp.bfloat16
    )
    come = send_group([vis_out] * GROUP, (1, GROUP))
    text_come = send_xor(text, (1, 2))
    far_cross_q = swap_cores(own)
    come, text_come, far_cross_q, own = after((come, text_come, far_cross_q, own_cross_o))
    scalars = [jnp.where(core == 0, small, far_small), jnp.where(core == 0, far_small, small)]

    image_parts = image_part([vis_out] + come, projector, own_cross_kv, far_cross_kv, begun)
    come = send_group(image_parts[0], (GROUP, GROUP))
    text = jnp.concatenate([text, text_come])
    text_come = send_xor(text, (2, 1))
    far_cross_o = swap_cores(own)
    come, text_come, far_cross_o, own = after((come, text_come, far_cross_o, own_self_kv))
    near = total([image_parts[0, 0]] + come).astype(jnp.bfloat16)
    come = send_group([near] * GROUP, (1, 1))
    gains = jnp.concatenate([text[:, rows:], text_come[:, rows:]])
    far_gains = swap_cores(gains)
    far_self_kv = swap_cores(own)
    gains = (gains, far_gains)
    text = [half[at : at + GROUP] for half in (text, text_come) for at in (0, GROUP)]
    queries = plain_query_part(0, 0, rows, text, gains, (own_cross_q, far_cross_q), text_mask)
    come, queries, far_self_kv = after((come, queries, far_self_kv))
    parts = [near] + come

    def image_rows(kv_rows, section):
        key_gain = scalars[section][1, HD : 2 * HD]
        near = jnp.concatenate(
            [rms_norm(kv_rows[:, :HD], key_gain), kv_rows[:, HD:]], axis=1
        ).astype(jnp.bfloat16)
        return near, swap_cores(near)

    near, far = image_rows(total(parts), 0)
    tile_rows = 2 * vision_states.shape[0] // TILES
    tiles = jnp.broadcast_to(visible_tiles[:, None], (seq_len, HD))
    cosine, sine = (jnp.asarray(table) for table in rope_tables(seq_len))

    def self_block(section, hidden, beside_mixed):
        nonlocal far_self_o
        steps = head_steps(key_value_part(section, hidden, scalars[section], own_self_kv, far_self_kv))
        come = send_group([hidden] * GROUP, (GROUP, 1))
        kv_rows = steps[1](steps[0]())
        extra = steps[2](kv_rows)
        come, kv_rows, extra = after((come, kv_rows, extra))
        if section == 0:
            far_self_o = swap_cores(own_self_o)
        first = jnp.stack([hidden] + come)
        come = send_group([first] * GROUP, (1, GROUP))
        kv_rows = steps[3](kv_rows, extra)
        kv_rows = steps[5](kv_rows, steps[4](kv_rows))
        extra = steps[6](kv_rows)
        if section == 0:
            come, kv_rows, extra, far_self_o = after((come, kv_rows, extra, far_self_o))
        else:
            come, kv_rows, extra = after((come, kv_rows, extra))
        near = steps[7](kv_rows, extra).astype(jnp.bfloat16)
        far = swap_cores(near)
        queries = query_part(
            section, 1, rows, [first] + come, gains, (own_self_q, far_self_q), cosine, sine
        )
        mixed = self_mix(full_width, queries, near, far, cosine, sine)
        pieces, extra = gather_chips(mixed, beside_mixed)
        hidden = out_part(
            section, False, pieces, hidden, scalars[section], tiles, own_self_o, far_self_o
        )
        return hidden, extra

    mixed = cross_mix(tile_rows, queries, near, far, tiles, scalars[0])
    mixed, own = after((mixed, own_self_q))
    pieces, far_self_q = gather_chips(mixed, lambda: swap_cores(own))
    hidden = out_part(0, True, pieces, hidden, scalars[0], tiles, own_cross_o, far_cross_o)
    far_self_o = None
    hidden, second_kept = after((hidden, image_parts[1]))
    second = head_steps(second_kept)

    def two_steps():
        second_rows = second[1](second[0]())
        return second_rows, second[2](second_rows)

    hidden, (second_rows, come) = self_block(0, hidden, two_steps)
    second_rows = second[3](second_rows, come)
    results = [hidden]

    hidden, second_rows = after((hidden, second_rows))
    come = second[4](second_rows)
    steps = send_group([hidden] * GROUP, (GROUP, 1))
    come, steps = after((come, steps))
    second_rows = second[5](second_rows, come)
    first = jnp.stack([hidden] + steps)
    come = second[6](second_rows)
    pieces = [first] + send_group([first] * GROUP, (1, GROUP))
    come, pieces = after((come, pieces))
    near, far = image_rows(second[7](second_rows, come), 1)
    queries = plain_query_part(1, 0, rows, pieces, gains, (own_cross_q, far_cross_q))
    mixed = cross_mix(tile_rows, queries, near, far, tiles, scalars[1])
    pieces, _ = gather_chips(mixed)
    hidden = out_part(1, True, pieces, hidden, scalars[1], tiles, own_cross_o, far_cross_o)
    hidden, _ = self_block(1, hidden, None)
    results.append(hidden)
    come = swap_cores(jnp.where(core == 0, results[1], results[0]))
    return jnp.where(
        core == 0,
        jnp.concatenate([results[0], come], axis=0),
        jnp.concatenate([come, results[1]], axis=0),
    )[None]


def solution(mesh):
    chips = mesh.shape["tp"]
    paired = mesh.shape["section"] == 2 and chips == GROUP * GROUP and HEADS == 2 * chips
    body = paired_body if paired else blocked_body
    in_specs = (
        P(None, "tp"),
        P("section", None),
        P(),
        P(),
        P(None, "tp"),
        P("tp", None),
        P(),
        P(None, "tp"),
        P("section", "tp"),
        P("section", None, "tp"),
        P("section", "tp", None),
        P("section", None, None),
        P("section", None, "tp"),
        P("section"),
        P("section", "tp"),
        P("section", None, "tp"),
        P("section", "tp", None),
        P("section", None, "tp"),
    )
    out_specs = P("section", None, "tp")
    return jax.shard_map(body, mesh=mesh, in_specs=in_specs, out_specs=out_specs, check_vma=False)
```
